128 devices in a mesh: clip: 32 (over y, x_hi, z), ha: 4 (over x_lo, core).
Axes of the slice: x: 4 (x_hi: 2, x_lo: 2; x = x_hi * 2 + x_lo), y: 4, z: 4, core: 2. Of those that a mesh axis runs over, the one named last changes fastest.
Arguments:
- frames: bfloat16 [120, 64, 32, 256], P(None, 'clip', 'ha'), may hold values from -6 to 6
- ln_gain: float32 [120], replicated, may hold values from 0.25 to 1.75
- w_qkv: bfloat16 [360, 120], replicated, may hold values from -4 to 4
- w_proj: bfloat16 [120, 240], replicated, may hold values from -0.375 to 0.375
- conv_weight: bfloat16 [2, 3, 3, 120, 120], replicated, may hold values from -0.1875 to 0.1875
Outputs:
- restored: bfloat16 [120, 64, 32, 256], P(None, 'clip', 'ha')
The draws below stay inside these ranges and needn't reach their ends.
All inputs are finite; a program needn't handle non-finite values.
Results may differ from the reference program's by a relative error of at most 0.012.
The reference program's roundings to bfloat16 on the way count: a program that leaves them out, or rounds other values in their place, can miss the bound.
Values may be sent and summed in bfloat16 or wider, within the bound.
A program may use at most 128 MiB of HBM per device.

```python
import jax
import jax.numpy as jnp
from jax import lax

C = 120
HEADS = 6
WIN = 8
W = 256
FRAMES = 64
H = 32


def draw_frames(key, part):
    key = jax.random.fold_in(key, 11)
    first = jax.random.fold_in(key, 0)
    values = jax.random.normal(first, (C, FRAMES, H, W), jnp.float32)
    return jnp.clip(values, -6.0, 6.0).astype(jnp.bfloat16)


def draw_w_qkv(key, part):
    key = jax.random.fold_in(key, 23)
    first = jax.random.fold_in(key, 0)
    values = jax.random.normal(first, (3 * C, C), jnp.float32) * C ** (-0.5)
    return jnp.clip(values, -4.0, 4.0).astype(jnp.bfloat16)


def bell_draw(key, dims, scale, most, kind=jnp.bfloat16):
    return jnp.clip(scale * jax.random.normal(key, dims, jnp.float32), -most, most).astype(kind)


def setup_inputs(seed: int = 0) -> dict:
    key_list = jax.random.split(jax.random.key(seed), 6)
    return {
        "frames": draw_frames(jax.random.fold_in(key_list[5], 71), 0),
        "ln_gain": jnp.clip(1.0 + 0.15 * jax.random.normal(key_list[1], (C,), jnp.float32), 0.25, 1.75),
        "w_qkv": draw_w_qkv(jax.random.fold_in(key_list[5], 71), 0),
        "w_proj": bell_draw(key_list[3], (C, 2 * C), (2 * C) ** -0.5, 0.375),
        "conv_weight": bell_draw(key_list[4], (2, 3, 3, C, C), (9 * C) ** -0.5, 0.1875),
    }


def layer_norm(frames, ln_gain):
    values = frames.astype(jnp.float32)
    average = lax.optimization_barrier(jnp.mean(values, axis=0, keepdims=True))
    spread = lax.optimization_barrier(jnp.mean((values - average) ** 2, axis=0, keepdims=True))
    normed = (values - average) * lax.rsqrt(spread + 1e-05) * ln_gain[:, None, None, None]
    return normed.astype(jnp.bfloat16)

def project(weight, field):
    return jnp.einsum('oi,ifhw->ofhw', weight.astype(jnp.float32), field.astype(jnp.float32))

def to_windows(field):
    c, f, h, w = field.shape
    d = c // HEADS
    shaped = field.reshape(HEADS, d, f // 2, 2, h // WIN, WIN, w // WIN, WIN)
    shaped = shaped.transpose(2, 4, 0, 6, 1, 3, 5, 7)
    return shaped.reshape(f // 2, h // WIN, HEADS, w // WIN, d, 2 * WIN * WIN)

def from_windows(blocks, c, f, h, w):
    d = c // HEADS
    shaped = blocks.reshape(f // 2, h // WIN, HEADS, w // WIN, d, 2, WIN, WIN)
    shaped = shaped.transpose(2, 4, 0, 5, 1, 6, 3, 7)
    return shaped.reshape(c, f, h, w)

def attend(queries, keys_all, values_all, usable):
    score_scale = queries.shape[-2] ** (-0.5)
    scores = jnp.einsum('...dq,...dk->...qk', queries.astype(jnp.float32), keys_all.astype(jnp.float32)) * score_scale
    scores = jnp.where(usable, scores, -1e+30)
    peak = lax.optimization_barrier(jnp.max(scores, axis=-1, keepdims=True))
    weights = jnp.exp(scores - peak)
    weights = (weights / lax.optimization_barrier(jnp.sum(weights, axis=-1, keepdims=True))).astype(jnp.bfloat16)
    result = jnp.einsum('...qk,...dk->...dq', weights.astype(jnp.float32), values_all.astype(jnp.float32))
    return result.astype(jnp.bfloat16)

def convolve(field, weight):
    rows = field.shape[2] - 2
    width = field.shape[3]
    padded = jnp.pad(field, ((0, 0), (0, 0), (0, 0), (1, 1)))
    total = jnp.zeros((weight.shape[2], field.shape[1], rows, width), jnp.float32)
    for row_off in range(3):
        for col_off in range(3):
            piece = padded[:, :, row_off:row_off + rows, col_off:col_off + width]
            total = total + jnp.einsum('oi,ifhw->ofhw', weight[row_off, col_off].astype(jnp.float32), piece.astype(jnp.float32))
    return total

def pad_rows(field):
    return jnp.pad(field, ((0, 0), (0, 0), (1, 1), (0, 0)))

def reference(frames, ln_gain, w_qkv, w_proj, conv_weight):
    c, f, h, w = frames.shape
    normed = layer_norm(frames, ln_gain)
    projected = project(w_qkv, normed).astype(jnp.bfloat16)
    query_win = to_windows(projected[:c])
    key_win = to_windows(projected[c:2 * c])
    value_win = to_windows(projected[2 * c:])
    clips = f // 2
    empty_clip = jnp.zeros_like(key_win[:1])
    key_prev = jnp.concatenate([empty_clip, key_win[:-1]], axis=0)
    key_next = jnp.concatenate([key_win[1:], empty_clip], axis=0)
    value_prev = jnp.concatenate([empty_clip, value_win[:-1]], axis=0)
    value_next = jnp.concatenate([value_win[1:], empty_clip], axis=0)
    tokens_win = 2 * WIN * WIN
    positions = jnp.arange(clips, dtype=jnp.int32)
    usable_mut = jnp.concatenate([jnp.broadcast_to((positions > 0)[:, None], (clips, tokens_win)), jnp.broadcast_to((positions < clips - 1)[:, None], (clips, tokens_win))], axis=1)
    usable_self = jnp.ones((tokens_win,), bool)

    def one_clip(members):
        queries, keys_own, values_own, keys_before, keys_later, values_before, values_later, usable = members
        self_part = attend(queries, keys_own, values_own, usable_self)
        keys_both = jnp.concatenate([keys_before, keys_later], axis=-1)
        values_both = jnp.concatenate([values_before, values_later], axis=-1)
        mutual_part = attend(queries, keys_both, values_both, usable)
        return (self_part, mutual_part)
    self_win, mutual_win = lax.map(one_clip, (query_win, key_win, value_win, key_prev, key_next, value_prev, value_next, usable_mut))
    self_out = from_windows(self_win, c, f, h, w)
    mutual_out = from_windows(mutual_win, c, f, h, w)
    joined = jnp.concatenate([self_out, mutual_out], axis=0)
    attended = (frames.astype(jnp.float32) + project(w_proj, joined)).astype(jnp.bfloat16)
    inner_act = jnp.maximum(convolve(pad_rows(attended), conv_weight[0]), 0.0).astype(jnp.bfloat16)
    restored = attended.astype(jnp.float32) + convolve(pad_rows(inner_act), conv_weight[1])
    return restored.astype(jnp.bfloat16)
```

```python
import functools
import math

import jax
import jax.numpy as jnp
from jax import lax
from jax.experimental import pallas as pl
from jax.experimental.pallas import tpu as pltpu
from jax.sharding import PartitionSpec as P

HEADS = 6
WIN = 8
C = 120
D = C // HEADS
CP = 128
DP = 32
TOK = 2 * WIN * WIN
CHUNKS = 4
HALO = 2
MESH = pl.DeviceIdType.MESH
F32 = jnp.float32
BF16 = jnp.bfloat16


def dot(a, b):
    return lax.dot_general(a, b, (((1,), (0,)), ((), ())), preferred_element_type=F32)


def dot_nt(a, b):
    return lax.dot_general(a, b, (((1,), (1,)), ((), ())), preferred_element_type=F32)


def iota(shape, dim):
    return lax.broadcasted_iota(jnp.int32, shape, dim)


def one_hot_heads(rows, cols, padded_dim):
    padded = iota((rows, cols), padded_dim)
    packed = iota((rows, cols), 1 - padded_dim)
    entry = padded & (DP - 1)
    hit = ((padded >> 5) * D + entry == packed) & (entry < D)
    return jnp.where(hit, 1.0, 0.0).astype(BF16)


def pad_rows(value, rows):
    extra = jnp.zeros((rows - value.shape[0], value.shape[1]), value.dtype)
    return jnp.concatenate([value, extra], axis=0)


def kernel(
    clips,
    parts,
    x_ref,
    gain_ref,
    wqkv_ref,
    wproj_ref,
    wconv_ref,
    out_ref,
    xn,
    xin,
    q_s,
    k_s,
    v_s,
    k2_s,
    v2_s,
    o_s,
    att,
    inner,
    wq_s,
    wk_s,
    wv_s,
    wp_s,
    wc_s,
    mask_s,
    left_s,
    right_s,
    send_sem,
    recv_sem,
    hsend_sem,
    hrecv_sem,
):
    me = lax.axis_index("clip")
    ha = lax.axis_index("ha")
    windows = x_ref.shape[0]
    per = windows // CHUNKS
    width = windows * WIN
    has_prev, has_next = me > 0, me < clips - 1
    has_up, has_down = ha > 0, ha < parts - 1

    att[...] = jnp.zeros_like(att)
    lane_one = jnp.where(iota((TOK, CP), 1) == C, 1.0, 0.0).astype(BF16)

    barrier = pltpu.get_barrier_semaphore()
    neighbours = (
        (has_prev, (me - 1, ha)),
        (has_next, (me + 1, ha)),
        (has_up, (me, ha - 1)),
        (has_down, (me, ha + 1)),
    )
    for there, device in neighbours:

        @pl.when(there)
        def _(device=device):
            pl.semaphore_signal(barrier, inc=1, device_id=device, device_id_type=MESH)

    wqkv = wqkv_ref[...].astype(F32)
    for slot, start in ((wq_s, 0), (wk_s, C)):
        slot[...] = jnp.zeros_like(slot)
        slot[:, :C] = pad_rows(wqkv[start : start + C], CP).astype(BF16)
    wv = dot(one_hot_heads(HEADS * DP, C, 0), wqkv[2 * C :].astype(BF16))
    ones_row = (iota((HEADS * DP, CP), 0) & (DP - 1) == D) & (iota((HEADS * DP, CP), 1) == C)
    wv_s[...] = jnp.where(ones_row, 1.0, 0.0).astype(BF16)
    wv_s[:, :C] = wv.astype(BF16)
    wp = dot(wproj_ref[...], one_hot_heads(2 * C, 2 * HEADS * DP, 1))
    wp_s[...] = pad_rows(wp, CP).astype(BF16)
    channel = iota((CP, TOK), 0)
    for h in range(HEADS):
        mask_s[h] = jnp.where((channel >= h * D) & (channel < (h + 1) * D), 1.0, 0.0).astype(BF16)

    gain = gain_ref[...]

    def norm_window(w, carry):
        x = x_ref[w].astype(F32)
        centred = x - jnp.mean(x, axis=-1, keepdims=True)
        spread = jnp.mean(centred * centred, axis=-1, keepdims=True)
        normed = centred * lax.rsqrt(spread + 1e-05) * gain
        xn[w] = lane_one
        xn[w, :, :C] = normed.astype(BF16)
        return carry

    def clip_copy(side, k):
        part = pl.ds(k * per, per)
        return pltpu.make_async_remote_copy(
            src_ref=xn.at[part],
            dst_ref=xin.at[side, part],
            send_sem=send_sem.at[side, k],
            recv_sem=recv_sem.at[side, k],
            device_id=(me + 1 - 2 * side, ha),
            device_id_type=MESH,
        )

    for k in range(CHUNKS):
        lax.fori_loop(k * per, (k + 1) * per, norm_window, 0, unroll=4)
        if k == 0:
            pl.semaphore_wait(barrier, sum(jnp.where(there, 1, 0) for there, _ in neighbours))

        @pl.when(has_next)
        def _(k=k):
            clip_copy(0, k).start()

        @pl.when(has_prev)
        def _(k=k):
            clip_copy(1, k).start()

    scale = math.log2(math.e) / math.sqrt(D)

    def attend(w, keys, values, first_row):
        q = q_s[w]
        for pair in range(HEADS // 2):
            queries = jnp.concatenate([q * mask_s[2 * pair], q * mask_s[2 * pair + 1]], axis=1)
            scores = dot(keys, queries)
            peak = jnp.max(scores, axis=0, keepdims=True)
            weights = jnp.exp2((scores - peak) * scale).astype(BF16)
            rows = pl.ds(2 * pair * DP, 2 * DP)
            got = dot(values[2 * pair * DP : 2 * (pair + 1) * DP], weights)
            for side in range(2):
                mine = got[side * DP : (side + 1) * DP, side * TOK : (side + 1) * TOK]
                mine = mine * (1.0 / mine[D : D + 1])
                start = first_row + (2 * pair + side) * DP
                o_s[w, start : start + DP] = mine.astype(BF16)

    def project_own(w, carry):
        x = xn[w]
        q_s[w] = dot_nt(wq_s[...], x).astype(BF16)
        k_s[w] = dot_nt(x, wk_s[...]).astype(BF16)
        v_s[w] = dot_nt(wv_s[...], x).astype(BF16)
        return carry

    lax.fori_loop(0, windows, project_own, 0, unroll=4)

    def self_window(w, carry):
        attend(w, k_s[w], v_s[w], 0)
        return carry

    lax.fori_loop(0, windows, self_window, 0, unroll=2)

    wc_s[...] = jnp.zeros_like(wc_s)
    for layer in range(2):
        for r in range(3):
            for s in range(3):
                weight = pad_rows(wconv_ref[layer, r, s].astype(F32), CP).astype(BF16)
                wc_s[layer, s * CP : (s + 1) * CP, r * CP : r * CP + C] = weight
    left_s[...] = jnp.zeros_like(left_s)
    right_s[...] = jnp.zeros_like(right_s)

    slot_prev = jnp.where(has_prev, 0, 1)
    slot_next = jnp.where(has_next, 1, 0)
    own_rows = x_ref.shape[1] // (2 * WIN)

    def project_both(w, carry):
        x = jnp.concatenate([xin[slot_prev, w], xin[slot_next, w]], axis=0)
        k2_s[w] = dot_nt(x, wk_s[...]).astype(BF16)
        v2_s[w] = dot_nt(wv_s[...], x).astype(BF16)
        return carry

    def mutual_window(w, carry):
        attend(w, k2_s[w], v2_s[w], HEADS * DP)
        return carry

    def finish_pair(p, carry):
        both = []
        for side in range(2):
            w = 2 * p + side
            mixed = dot(wp_s[...], o_s[w]).T
            both.append(x_ref[w].astype(F32) + mixed[:, :C])
        shaped = jnp.stack(both, axis=0).reshape(2, 2, own_rows, WIN, C)
        shaped = shaped.transpose(1, 2, 0, 3, 4).reshape(2, own_rows, 2 * WIN, C)
        cols = pl.ds(pl.multiple_of(p * 2 * WIN, 2 * WIN), 2 * WIN)
        att[:, HALO : HALO + own_rows, cols, :C] = shaped.astype(BF16)
        return carry

    def halo_copy(side, k):
        cols = pl.ds(k * per * WIN, per * WIN)
        src_row = own_rows if side else HALO
        dst_row = 0 if side else HALO + own_rows
        return pltpu.make_async_remote_copy(
            src_ref=att.at[:, pl.ds(src_row, HALO), cols],
            dst_ref=att.at[:, pl.ds(dst_row, HALO), cols],
            send_sem=hsend_sem.at[side, k],
            recv_sem=hrecv_sem.at[side, k],
            device_id=(me, ha + (1 if side else -1)),
            device_id_type=MESH,
        )

    for k in range(CHUNKS):

        @pl.when(has_prev)
        def _(k=k):
            clip_copy(0, k).wait_recv()

        @pl.when(has_next)
        def _(k=k):
            clip_copy(1, k).wait_recv()

        lax.fori_loop(k * per, (k + 1) * per, project_both, 0, unroll=4)
        lax.fori_loop(k * per, (k + 1) * per, mutual_window, 0, unroll=2)
        lax.fori_loop(k * per // 2, (k + 1) * per // 2, finish_pair, 0, unroll=2)

        @pl.when(has_up)
        def _(k=k):
            halo_copy(0, k).start()

        @pl.when(has_down)
        def _(k=k):
            halo_copy(1, k).start()

    def convolve(field, row, layer, f):
        stacked = jnp.concatenate([field[f, row], field[f, row + 1], field[f, row + 2]], axis=1)
        part = dot_nt(stacked, wc_s[layer])
        left_s[f, 8 : 8 + width] = part[:, :CP]
        right_s[f, 0:width] = part[:, 2 * CP :]
        return part[:, CP : 2 * CP] + left_s[f, 7 : 7 + width] + right_s[f, 1 : 1 + width]

    def first_conv(row, carry):
        for f in range(2):
            inner[f, row] = jnp.maximum(convolve(att, row, 0, f), 0.0).astype(BF16)
        return carry

    def second_conv(row, carry):
        for f in range(2):
            total = att[f, row + HALO].astype(F32) + convolve(inner, row, 1, f)
            out_ref[f, row] = total[:, :C].astype(BF16)
        return carry

    lax.fori_loop(HALO, own_rows, first_conv, 0)
    for k in range(CHUNKS):

        @pl.when(has_down)
        def _(k=k):
            halo_copy(0, k).wait_recv()

        @pl.when(has_up)
        def _(k=k):
            halo_copy(1, k).wait_recv()

    lax.fori_loop(0, HALO, first_conv, 0)
    lax.fori_loop(own_rows, own_rows + HALO, first_conv, 0)

    @pl.when(jnp.logical_not(has_up))
    def _():
        inner[:, 0] = jnp.zeros_like(inner[:, 0])

    @pl.when(jnp.logical_not(has_down))
    def _():
        inner[:, own_rows + 1] = jnp.zeros_like(inner[:, 0])

    lax.fori_loop(0, own_rows, second_conv, 0)

    for k in range(CHUNKS):
        for copy, low, high in ((clip_copy, has_next, has_prev), (halo_copy, has_up, has_down)):

            @pl.when(low)
            def _(copy=copy, k=k):
                copy(0, k).wait_send()

            @pl.when(high)
            def _(copy=copy, k=k):
                copy(1, k).wait_send()


def shards(frames, ln_gain, w_qkv, w_proj, conv_weight):
    c, f, h, w = frames.shape
    windows = w // WIN
    clips, parts = lax.axis_size("clip"), lax.axis_size("ha")
    tokens = frames.reshape(c, f, h, windows, WIN).transpose(3, 1, 2, 4, 0)
    tokens = tokens.reshape(windows, f * h * WIN, c)
    vmem = pl.BlockSpec(memory_space=pltpu.VMEM)
    restored = pl.pallas_call(
        functools.partial(kernel, clips, parts),
        out_shape=jax.ShapeDtypeStruct((f, h, w, c), BF16),
        in_specs=[vmem] * 5,
        out_specs=vmem,
        scratch_shapes=[
            pltpu.VMEM((windows, TOK, CP), BF16),
            pltpu.VMEM((2, windows, TOK, CP), BF16),
            pltpu.VMEM((windows, CP, TOK), BF16),
            pltpu.VMEM((windows, TOK, CP), BF16),
            pltpu.VMEM((windows, HEADS * DP, TOK), BF16),
            pltpu.VMEM((windows, 2 * TOK, CP), BF16),
            pltpu.VMEM((windows, HEADS * DP, 2 * TOK), BF16),
            pltpu.VMEM((windows, 2 * HEADS * DP, TOK), BF16),
            pltpu.VMEM((f, h + 2 * HALO, w, CP), BF16),
            pltpu.VMEM((f, h + 2, w, CP), BF16),
            pltpu.VMEM((CP, CP), BF16),
            pltpu.VMEM((CP, CP), BF16),
            pltpu.VMEM((HEADS * DP, CP), BF16),
            pltpu.VMEM((CP, 2 * HEADS * DP), BF16),
            pltpu.VMEM((2, 3 * CP, 3 * CP), BF16),
            pltpu.VMEM((HEADS, CP, TOK), BF16),
            pltpu.VMEM((f, w + 16, CP), F32),
            pltpu.VMEM((f, w + 16, CP), F32),
            pltpu.SemaphoreType.DMA((2, CHUNKS)),
            pltpu.SemaphoreType.DMA((2, CHUNKS)),
            pltpu.SemaphoreType.DMA((2, CHUNKS)),
            pltpu.SemaphoreType.DMA((2, CHUNKS)),
        ],
        compiler_params=pltpu.CompilerParams(
            collective_id=0, has_side_effects=True, vmem_limit_bytes=48 * 1024 * 1024
        ),
    )(tokens, ln_gain.reshape(1, c), w_qkv, w_proj, conv_weight)
    return restored.transpose(3, 0, 1, 2)


def solution(mesh):
    return jax.shard_map(
        shards,
        mesh=mesh,
        in_specs=(P(None, "clip", "ha", None), P(), P(), P(), P()),
        out_specs=P(None, "clip", "ha", None),
        check_vma=False,
    )
```

```python
import functools
import math

import jax
import jax.numpy as jnp
from jax import lax
from jax.experimental import pallas as pl
from jax.experimental.pallas import tpu as pltpu
from jax.sharding import PartitionSpec as P

HEADS = 6
WIN = 8
C = 120
D = C // HEADS
CP = 128
DP = 32
TOK = 2 * WIN * WIN
CHUNKS = 4
HALO = 2
GROUP = 4
PROJ = 8
FIN = 8
ROWS = 2
MESH = pl.DeviceIdType.MESH
F32 = jnp.float32
BF16 = jnp.bfloat16


def dot(a, b):
    return lax.dot_general(a, b, (((1,), (0,)), ((), ())), preferred_element_type=F32)


def dot_nt(a, b):
    return lax.dot_general(a, b, (((1,), (1,)), ((), ())), preferred_element_type=F32)


def iota(shape, dim):
    return lax.broadcasted_iota(jnp.int32, shape, dim)


def one_hot_heads(rows, cols, padded_dim):
    padded = iota((rows, cols), padded_dim)
    packed = iota((rows, cols), 1 - padded_dim)
    entry = padded & (DP - 1)
    hit = ((padded >> 5) * D + entry == packed) & (entry < D)
    return jnp.where(hit, 1.0, 0.0).astype(BF16)


def pad_rows(value, rows):
    extra = jnp.zeros((rows - value.shape[0], value.shape[1]), value.dtype)
    return jnp.concatenate([value, extra], axis=0)


def kernel(
    clips,
    parts,
    x_ref,
    gain_ref,
    wqkv_ref,
    wproj_ref,
    wconv_ref,
    out_ref,
    xn,
    xin,
    q_s,
    k_s,
    v_s,
    k2_s,
    v2_s,
    o_s,
    att,
    inner,
    wq_s,
    wk_s,
    wv_s,
    wp_s,
    wc_s,
    mask_s,
    left_s,
    right_s,
    send_sem,
    recv_sem,
    hsend_sem,
    hrecv_sem,
):
    me = lax.axis_index("clip")
    ha = lax.axis_index("ha")
    windows = x_ref.shape[0]
    per = windows // CHUNKS
    width = windows * WIN
    has_prev, has_next = me > 0, me < clips - 1
    has_up, has_down = ha > 0, ha < parts - 1

    att[...] = jnp.zeros_like(att)
    lane_one = jnp.where(iota((TOK, CP), 1) == C, 1.0, 0.0).astype(BF16)

    barrier = pltpu.get_barrier_semaphore()
    neighbours = (
        (has_prev, (me - 1, ha)),
        (has_next, (me + 1, ha)),
        (has_up, (me, ha - 1)),
        (has_down, (me, ha + 1)),
    )
    for there, device in neighbours:

        @pl.when(there)
        def _(device=device):
            pl.semaphore_signal(barrier, inc=1, device_id=device, device_id_type=MESH)

    wqkv = wqkv_ref[...].astype(F32)
    for slot, start in ((wq_s, 0), (wk_s, C)):
        slot[...] = jnp.zeros_like(slot)
        slot[:, :C] = pad_rows(wqkv[start : start + C], CP).astype(BF16)
    wv = dot(one_hot_heads(HEADS * DP, C, 0), wqkv[2 * C :].astype(BF16))
    ones_row = (iota((HEADS * DP, CP), 0) & (DP - 1) == D) & (iota((HEADS * DP, CP), 1) == C)
    wv_s[...] = jnp.where(ones_row, 1.0, 0.0).astype(BF16)
    wv_s[:, :C] = wv.astype(BF16)
    wp = dot(wproj_ref[...], one_hot_heads(2 * C, 2 * HEADS * DP, 1))
    wp_s[...] = pad_rows(wp, CP).astype(BF16)
    channel = iota((CP, TOK), 0)
    for h in range(HEADS):
        mask_s[h] = jnp.where((channel >= h * D) & (channel < (h + 1) * D), 1.0, 0.0).astype(BF16)

    gain = gain_ref[...]

    def norm_window(w, carry):
        x = x_ref[w].astype(F32)
        centred = x - jnp.mean(x, axis=-1, keepdims=True)
        spread = jnp.mean(centred * centred, axis=-1, keepdims=True)
        normed = centred * lax.rsqrt(spread + 1e-05) * gain
        xn[w] = lane_one
        xn[w, :, :C] = normed.astype(BF16)
        return carry

    def clip_copy(side, k):
        part = pl.ds(k * per, per)
        return pltpu.make_async_remote_copy(
            src_ref=xn.at[part],
            dst_ref=xin.at[side, part],
            send_sem=send_sem.at[side, k],
            recv_sem=recv_sem.at[side, k],
            device_id=(me + 1 - 2 * side, ha),
            device_id_type=MESH,
        )

    for k in range(CHUNKS):
        lax.fori_loop(k * per, (k + 1) * per, norm_window, 0, unroll=4)
        if k == 0:
            pl.semaphore_wait(barrier, sum(jnp.where(there, 1, 0) for there, _ in neighbours))

        @pl.when(has_next)
        def _(k=k):
            clip_copy(0, k).start()

        @pl.when(has_prev)
        def _(k=k):
            clip_copy(1, k).start()

    scale = math.log2(math.e) / math.sqrt(D)

    def attend(ws, keys, values, first_row):
        jobs = [(w, pair) for w in range(len(ws)) for pair in range(HEADS // 2)]
        qs = [q_s[w] for w in ws]
        scores = [
            dot(
                keys[w],
                jnp.concatenate([qs[w] * mask_s[2 * pair], qs[w] * mask_s[2 * pair + 1]], axis=1),
            )
            for w, pair in jobs
        ]
        weights = []
        for score in scores:
            peak = jnp.max(score, axis=0, keepdims=True)
            weights.append(jnp.exp2((score - peak) * scale).astype(BF16))
        gots = [
            dot(values[w][2 * pair * DP : 2 * (pair + 1) * DP], weight)
            for (w, pair), weight in zip(jobs, weights)
        ]
        for (w, pair), got in zip(jobs, gots):
            for side in range(2):
                mine = got[side * DP : (side + 1) * DP, side * TOK : (side + 1) * TOK]
                mine = mine * (1.0 / mine[D : D + 1])
                start = first_row + (2 * pair + side) * DP
                o_s[ws[w], start : start + DP] = mine.astype(BF16)

    def project_own(g, carry):
        ws = pl.ds(g * PROJ, PROJ)
        x = xn[ws].reshape(PROJ * TOK, CP)
        k_s[ws] = dot_nt(x, wk_s[...]).astype(BF16).reshape(PROJ, TOK, CP)
        q = dot_nt(wq_s[...], x).astype(BF16)
        v = dot_nt(wv_s[...], x).astype(BF16)
        for i in range(PROJ):
            q_s[g * PROJ + i] = q[:, i * TOK : (i + 1) * TOK]
            v_s[g * PROJ + i] = v[:, i * TOK : (i + 1) * TOK]
        return carry

    lax.fori_loop(0, windows // PROJ, project_own, 0)

    def self_window(g, carry):
        ws = [g * GROUP + i for i in range(GROUP)]
        attend(ws, [k_s[w] for w in ws], [v_s[w] for w in ws], 0)
        return carry

    lax.fori_loop(0, windows // GROUP, self_window, 0)

    wc_s[...] = jnp.zeros_like(wc_s)
    for layer in range(2):
        for r in range(3):
            for s in range(3):
                weight = pad_rows(wconv_ref[layer, r, s].astype(F32), CP).astype(BF16)
                wc_s[layer, s * CP : (s + 1) * CP, r * CP : r * CP + C] = weight
    left_s[...] = jnp.zeros_like(left_s)
    right_s[...] = jnp.zeros_like(right_s)

    slot_prev = jnp.where(has_prev, 0, 1)
    slot_next = jnp.where(has_next, 1, 0)
    own_rows = x_ref.shape[1] // (2 * WIN)

    def project_both(g, carry):
        ws = pl.ds(g * PROJ, PROJ)
        for side, slot in ((0, slot_prev), (1, slot_next)):
            x = xin[slot, ws].reshape(PROJ * TOK, CP)
            part = pl.ds(side * TOK, TOK)
            k2_s[ws, part] = dot_nt(x, wk_s[...]).astype(BF16).reshape(PROJ, TOK, CP)
            v = dot_nt(wv_s[...], x).astype(BF16)
            for i in range(PROJ):
                v2_s[g * PROJ + i, :, part] = v[:, i * TOK : (i + 1) * TOK]
        return carry

    def mutual_window(g, carry):
        ws = [g * GROUP + i for i in range(GROUP)]
        attend(ws, [k2_s[w] for w in ws], [v2_s[w] for w in ws], HEADS * DP)
        return carry

    def finish_pair(g, carry):
        ws = [g * FIN + i for i in range(FIN)]
        mixed = [dot(wp_s[...], o_s[w]) for w in ws]
        mixed = [m.T[:, :C] for m in mixed]
        for i in range(0, FIN, 2):
            both = [x_ref[ws[i + j]].astype(F32) + mixed[i + j] for j in range(2)]
            shaped = jnp.stack(both, axis=0).reshape(2, 2, own_rows, WIN, C)
            shaped = shaped.transpose(1, 2, 0, 3, 4).reshape(2, own_rows, 2 * WIN, C)
            cols = pl.ds(pl.multiple_of((g * FIN + i) * WIN, 2 * WIN), 2 * WIN)
            att[:, HALO : HALO + own_rows, cols, :C] = shaped.astype(BF16)
        return carry

    def halo_copy(side, k):
        cols = pl.ds(k * per * WIN, per * WIN)
        src_row = own_rows if side else HALO
        dst_row = 0 if side else HALO + own_rows
        return pltpu.make_async_remote_copy(
            src_ref=att.at[:, pl.ds(src_row, HALO), cols],
            dst_ref=att.at[:, pl.ds(dst_row, HALO), cols],
            send_sem=hsend_sem.at[side, k],
            recv_sem=hrecv_sem.at[side, k],
            device_id=(me, ha + (1 if side else -1)),
            device_id_type=MESH,
        )

    for k in range(CHUNKS):

        @pl.when(has_prev)
        def _(k=k):
            clip_copy(0, k).wait_recv()

        @pl.when(has_next)
        def _(k=k):
            clip_copy(1, k).wait_recv()

        lax.fori_loop(k * per // PROJ, (k + 1) * per // PROJ, project_both, 0)
        lax.fori_loop(k * per // GROUP, (k + 1) * per // GROUP, mutual_window, 0)
        lax.fori_loop(k * per // FIN, (k + 1) * per // FIN, finish_pair, 0)

        @pl.when(has_up)
        def _(k=k):
            halo_copy(0, k).start()

        @pl.when(has_down)
        def _(k=k):
            halo_copy(1, k).start()

    def convolve(field, jobs, layer):
        stacked = jnp.concatenate(
            [
                jnp.concatenate([field[f, row + r] for r in range(3)], axis=1)
                for f, row in jobs
            ],
            axis=0,
        )
        part = dot_nt(stacked, wc_s[layer])
        for i in range(len(jobs)):
            mine = part[i * width : (i + 1) * width]
            left_s[i, 8 : 8 + width] = mine[:, :CP]
            right_s[i, 0:width] = mine[:, 2 * CP :]
        return [
            part[i * width : (i + 1) * width, CP : 2 * CP]
            + left_s[i, 7 : 7 + width]
            + right_s[i, 1 : 1 + width]
            for i in range(len(jobs))
        ]

    def conv_jobs(group):
        return [(f, group * ROWS + i) for i in range(ROWS) for f in range(2)]

    def first_conv(group, carry):
        jobs = conv_jobs(group)
        for (f, row), total in zip(jobs, convolve(att, jobs, 0)):
            inner[f, row] = jnp.maximum(total, 0.0).astype(BF16)
        return carry

    def second_conv(group, carry):
        jobs = conv_jobs(group)
        for (f, row), total in zip(jobs, convolve(inner, jobs, 1)):
            total = att[f, row + HALO].astype(F32) + total
            out_ref[f, row] = total[:, :C].astype(BF16)
        return carry

    lax.fori_loop(HALO // ROWS, own_rows // ROWS, first_conv, 0)
    for k in range(CHUNKS):

        @pl.when(has_down)
        def _(k=k):
            halo_copy(0, k).wait_recv()

        @pl.when(has_up)
        def _(k=k):
            halo_copy(1, k).wait_recv()

    lax.fori_loop(0, HALO // ROWS, first_conv, 0)
    lax.fori_loop(own_rows // ROWS, (own_rows + HALO) // ROWS, first_conv, 0)

    @pl.when(jnp.logical_not(has_up))
    def _():
        inner[:, 0] = jnp.zeros_like(inner[:, 0])

    @pl.when(jnp.logical_not(has_down))
    def _():
        inner[:, own_rows + 1] = jnp.zeros_like(inner[:, 0])

    lax.fori_loop(0, own_rows // ROWS, second_conv, 0)

    for k in range(CHUNKS):
        for copy, low, high in ((clip_copy, has_next, has_prev), (halo_copy, has_up, has_down)):

            @pl.when(low)
            def _(copy=copy, k=k):
                copy(0, k).wait_send()

            @pl.when(high)
            def _(copy=copy, k=k):
                copy(1, k).wait_send()


def shards(frames, ln_gain, w_qkv, w_proj, conv_weight):
    c, f, h, w = frames.shape
    windows = w // WIN
    clips, parts = lax.axis_size("clip"), lax.axis_size("ha")
    tokens = frames.reshape(c, f, h, windows, WIN).transpose(3, 1, 2, 4, 0)
    tokens = tokens.reshape(windows, f * h * WIN, c)
    vmem = pl.BlockSpec(memory_space=pltpu.VMEM)
    restored = pl.pallas_call(
        functools.partial(kernel, clips, parts),
        out_shape=jax.ShapeDtypeStruct((f, h, w, c), BF16),
        in_specs=[vmem] * 5,
        out_specs=vmem,
        scratch_shapes=[
            pltpu.VMEM((windows, TOK, CP), BF16),
            pltpu.VMEM((2, windows, TOK, CP), BF16),
            pltpu.VMEM((windows, CP, TOK), BF16),
            pltpu.VMEM((windows, TOK, CP), BF16),
            pltpu.VMEM((windows, HEADS * DP, TOK), BF16),
            pltpu.VMEM((windows, 2 * TOK, CP), BF16),
            pltpu.VMEM((windows, HEADS * DP, 2 * TOK), BF16),
            pltpu.VMEM((windows, 2 * HEADS * DP, TOK), BF16),
            pltpu.VMEM((f, h + 2 * HALO, w, CP), BF16),
            pltpu.VMEM((f, h + 2, w, CP), BF16),
            pltpu.VMEM((CP, CP), BF16),
            pltpu.VMEM((CP, CP), BF16),
            pltpu.VMEM((HEADS * DP, CP), BF16),
            pltpu.VMEM((CP, 2 * HEADS * DP), BF16),
            pltpu.VMEM((2, 3 * CP, 3 * CP), BF16),
            pltpu.VMEM((HEADS, CP, TOK), BF16),
            pltpu.VMEM((2 * ROWS, w + 16, CP), F32),
            pltpu.VMEM((2 * ROWS, w + 16, CP), F32),
            pltpu.SemaphoreType.DMA((2, CHUNKS)),
            pltpu.SemaphoreType.DMA((2, CHUNKS)),
            pltpu.SemaphoreType.DMA((2, CHUNKS)),
            pltpu.SemaphoreType.DMA((2, CHUNKS)),
        ],
        compiler_params=pltpu.CompilerParams(
            collective_id=0, has_side_effects=True, vmem_limit_bytes=48 * 1024 * 1024
        ),
    )(tokens, ln_gain.reshape(1, c), w_qkv, w_proj, conv_weight)
    return restored.transpose(3, 0, 1, 2)


def solution(mesh):
    return jax.shard_map(
        shards,
        mesh=mesh,
        in_specs=(P(None, "clip", "ha", None), P(), P(), P(), P()),
        out_specs=P(None, "clip", "ha", None),
        check_vma=False,
    )
```

```python
import functools
import math

import jax
import jax.numpy as jnp
from jax import lax
from jax.experimental import pallas as pl
from jax.experimental.pallas import tpu as pltpu
from jax.sharding import PartitionSpec as P

HEADS = 6
WIN = 8
C = 120
D = C // HEADS
CP = 128
DP = 32
TOK = 2 * WIN * WIN
HALO = 2
CUTS = (8, 8, 8, 4, 4)
GROUP = 8
LAG = 16
LAG1 = 4
LAG2 = 6
LAG3 = 8
MESH = pl.DeviceIdType.MESH
F32 = jnp.float32
BF16 = jnp.bfloat16


def dot(a, b):
    return lax.dot_general(a, b, (((1,), (0,)), ((), ())), preferred_element_type=F32)


def dot_nt(a, b):
    return lax.dot_general(a, b, (((1,), (1,)), ((), ())), preferred_element_type=F32)


def iota(shape, dim):
    return lax.broadcasted_iota(jnp.int32, shape, dim)


def one_hot_heads(rows, cols, padded_dim):
    padded = iota((rows, cols), padded_dim)
    packed = iota((rows, cols), 1 - padded_dim)
    entry = padded & (DP - 1)
    hit = ((padded >> 5) * D + entry == packed) & (entry < D)
    return jnp.where(hit, 1.0, 0.0).astype(BF16)


def pad_rows(value, rows):
    extra = jnp.zeros((rows - value.shape[0], value.shape[1]), value.dtype)
    return jnp.concatenate([value, extra], axis=0)


def kernel(
    clips,
    parts,
    x_ref,
    gain_ref,
    wqkv_ref,
    wproj_ref,
    wconv_ref,
    out_ref,
    xn,
    xin,
    q_s,
    k_s,
    v_s,
    k2_s,
    v2_s,
    o_s,
    att,
    inner,
    wq_s,
    wk_s,
    wv_s,
    wp_s,
    wc_s,
    mask_s,
    left1_s,
    middle1_s,
    right1_s,
    left2_s,
    middle2_s,
    right2_s,
    wconv_s,
    weights_sem,
    send_sem,
    recv_sem,
    hsend_sem,
    hrecv_sem,
):
    me = lax.axis_index("clip")
    ha = lax.axis_index("ha")
    width = x_ref.shape[2]
    windows = width // WIN
    own_rows = x_ref.shape[1]
    spans = []
    for size in CUTS:
        start = sum(CUTS[: len(spans)])
        spans.append((start, start + size))
    has_prev, has_next = me > 0, me < clips - 1
    has_up, has_down = ha > 0, ha < parts - 1

    weights_copy = pltpu.make_async_copy(wconv_ref, wconv_s, weights_sem)
    weights_copy.start()
    att[...] = jnp.zeros_like(att)
    lane_one = jnp.where(iota((TOK, CP), 1) == C, 1.0, 0.0).astype(BF16)

    barrier = pltpu.get_barrier_semaphore()
    neighbours = (
        (has_prev, (me - 1, ha)),
        (has_next, (me + 1, ha)),
        (has_up, (me, ha - 1)),
        (has_down, (me, ha + 1)),
    )
    for there, device in neighbours:

        @pl.when(there)
        def _(device=device):
            pl.semaphore_signal(barrier, inc=1, device_id=device, device_id_type=MESH)

    wqkv = wqkv_ref[...].astype(F32)
    for slot, start in ((wq_s, 0), (wk_s, C)):
        slot[...] = jnp.zeros_like(slot)
        slot[:, :C] = pad_rows(wqkv[start : start + C], CP).astype(BF16)
    wv = dot(one_hot_heads(HEADS * DP, C, 0), wqkv[2 * C :].astype(BF16))
    ones_row = (iota((HEADS * DP, CP), 0) & (DP - 1) == D) & (iota((HEADS * DP, CP), 1) == C)
    wv_s[...] = jnp.where(ones_row, 1.0, 0.0).astype(BF16)
    wv_s[:, :C] = wv.astype(BF16)
    wp = dot(wproj_ref[...], one_hot_heads(2 * C, 2 * HEADS * DP, 1))
    wp_s[...] = pad_rows(wp, CP).astype(BF16)
    channel = iota((CP, TOK), 0)
    for h in range(HEADS):
        mask_s[h] = jnp.where((channel >= h * D) & (channel < (h + 1) * D), 1.0, 0.0).astype(BF16)

    gain = gain_ref[...]

    def norm_pair(p, carry):
        cols = pl.ds(pl.multiple_of(p * 2 * WIN, 2 * WIN), 2 * WIN)
        x = x_ref[:, :, cols].astype(F32).reshape(2, own_rows, 2, WIN, C)
        x = x.transpose(2, 0, 1, 3, 4).reshape(2, TOK, C)
        centred = x - jnp.mean(x, axis=-1, keepdims=True)
        spread = jnp.mean(centred * centred, axis=-1, keepdims=True)
        normed = centred * lax.rsqrt(spread + 1e-05) * gain
        for i in range(2):
            xn[2 * p + i] = lane_one
        xn[pl.ds(2 * p, 2), :, :C] = normed.astype(BF16)
        return carry

    def clip_copy(side, k):
        first, last = spans[k]
        part = pl.ds(first, last - first)
        return pltpu.make_async_remote_copy(
            src_ref=xn.at[part],
            dst_ref=xin.at[side, part],
            send_sem=send_sem.at[side, k],
            recv_sem=recv_sem.at[side, k],
            device_id=(me + 1 - 2 * side, ha),
            device_id_type=MESH,
        )

    for k, (first, last) in enumerate(spans):
        lax.fori_loop(first // 2, last // 2, norm_pair, 0, unroll=2)
        if k == 0:
            pl.semaphore_wait(barrier, sum(jnp.where(there, 1, 0) for there, _ in neighbours))

        @pl.when(has_next)
        def _(k=k):
            clip_copy(0, k).start()

        @pl.when(has_prev)
        def _(k=k):
            clip_copy(1, k).start()

    scale = math.log2(math.e) / math.sqrt(D)

    def attend(ws, keys, values, first_row):
        jobs = [(w, pair) for w in range(len(ws)) for pair in range(HEADS // 2)]
        qs = [q_s[w] for w in ws]
        scores, weights, gots = {}, {}, {}

        def score(j):
            w, pair = jobs[j]
            queries = jnp.concatenate(
                [qs[w] * mask_s[2 * pair], qs[w] * mask_s[2 * pair + 1]], axis=1
            )
            scores[j] = dot(keys[w], queries)

        def weigh(j):
            got = scores.pop(j)
            peak = jnp.max(got, axis=0, keepdims=True)
            weights[j] = jnp.exp2((got - peak) * scale).astype(BF16)

        def gather(j):
            w, pair = jobs[j]
            gots[j] = dot(values[w][2 * pair * DP : 2 * (pair + 1) * DP], weights.pop(j))

        def store(j):
            w, pair = jobs[j]
            got = gots.pop(j)
            for side in range(2):
                mine = got[side * DP : (side + 1) * DP, side * TOK : (side + 1) * TOK]
                mine = mine * (1.0 / mine[D : D + 1])
                start = first_row + (2 * pair + side) * DP
                o_s[ws[w], start : start + DP] = mine.astype(BF16)

        n = len(jobs)
        for t in range(n + LAG2 + LAG3):
            if t < n:
                score(t)
            if 0 <= t - LAG1 < n:
                weigh(t - LAG1)
            if 0 <= t - LAG2 < n:
                gather(t - LAG2)
            if 0 <= t - LAG3 < n:
                store(t - LAG3)

    def project_own(g, carry):
        ws = pl.ds(g * GROUP, GROUP)
        x = xn[ws].reshape(GROUP * TOK, CP)
        k_s[ws] = dot_nt(x, wk_s[...]).astype(BF16).reshape(GROUP, TOK, CP)
        q = dot_nt(wq_s[...], x).astype(BF16)
        v = dot_nt(wv_s[...], x).astype(BF16)
        for i in range(GROUP):
            q_s[g * GROUP + i] = q[:, i * TOK : (i + 1) * TOK]
            v_s[g * GROUP + i] = v[:, i * TOK : (i + 1) * TOK]
        return carry

    lax.fori_loop(0, windows // GROUP, project_own, 0)

    def self_window(g, carry):
        ws = [g * GROUP + i for i in range(GROUP)]
        attend(ws, [k_s[w] for w in ws], [v_s[w] for w in ws], 0)
        return carry

    lax.fori_loop(0, windows // GROUP, self_window, 0)

    weights_copy.wait()
    wc_s[...] = jnp.zeros_like(wc_s)
    for layer in range(2):
        for r in range(3):
            for s in range(3):
                weight = pad_rows(wconv_s[layer, r, s].astype(F32), CP).astype(BF16)
                wc_s[layer, s * CP : (s + 1) * CP, r * CP : r * CP + C] = weight
    for slot, row in ((left1_s, 0), (left2_s, 0), (right1_s, width), (right2_s, width)):
        slot[:, row : row + 8] = jnp.zeros((slot.shape[0], 8, CP), F32)

    slot_prev = jnp.where(has_prev, 0, 1)
    slot_next = jnp.where(has_next, 1, 0)

    def mutual_chunk(first, last):
        ws = pl.ds(first, last - first)
        for side, slot in ((0, slot_prev), (1, slot_next)):
            x = xin[slot, ws].reshape((last - first) * TOK, CP)
            part = slice(side * TOK, (side + 1) * TOK)
            k2_s[ws, part] = dot_nt(x, wk_s[...]).astype(BF16).reshape(last - first, TOK, CP)
            v = dot_nt(wv_s[...], x).astype(BF16)
            for i in range(last - first):
                v2_s[first + i, :, part] = v[:, i * TOK : (i + 1) * TOK]
        every = list(range(first, last))
        attend(every, [k2_s[w] for w in every], [v2_s[w] for w in every], HEADS * DP)
        mixed = [dot(wp_s[...], o_s[w]) for w in every]
        mixed = [m.T[:, :C] for m in mixed]
        for i in range(0, len(every), 2):
            shaped = jnp.stack(mixed[i : i + 2], axis=0).reshape(2, 2, own_rows, WIN, C)
            shaped = shaped.transpose(1, 2, 0, 3, 4).reshape(2, own_rows, 2 * WIN, C)
            cols = slice(every[i] * WIN, every[i] * WIN + 2 * WIN)
            total = x_ref[:, :, cols].astype(F32) + shaped
            att[:, HALO : HALO + own_rows, cols, :C] = total.astype(BF16)

    def halo_copy(side, k):
        first, last = spans[k]
        cols = pl.ds(first * WIN, (last - first) * WIN)
        src_row = own_rows if side else HALO
        dst_row = 0 if side else HALO + own_rows
        return pltpu.make_async_remote_copy(
            src_ref=att.at[:, pl.ds(src_row, HALO), cols],
            dst_ref=att.at[:, pl.ds(dst_row, HALO), cols],
            send_sem=hsend_sem.at[side, k],
            recv_sem=hrecv_sem.at[side, k],
            device_id=(me, ha + (1 if side else -1)),
            device_id_type=MESH,
        )

    def products(field, jobs, layer, slots, start, stop):
        stacked = jnp.concatenate(
            [
                jnp.concatenate([field[f, row + r, start:stop] for r in range(3)], axis=1)
                for f, row in jobs
            ],
            axis=0,
        )
        part = dot_nt(stacked, wc_s[layer])
        size = stop - start
        left, middle, right = slots
        for i, (f, row) in enumerate(jobs):
            job = f * (own_rows + 2) + row
            mine = part[i * size : (i + 1) * size]
            left[job, 8 + start : 8 + stop] = mine[:, :CP]
            middle[job, start:stop] = mine[:, CP : 2 * CP]
            right[job, start:stop] = mine[:, 2 * CP :]

    def summed(slots, f, row, start, stop):
        left, middle, right = slots
        job = f * (own_rows + 2) + row
        return (
            middle[job, start:stop]
            + left[job, 7 + start : 7 + stop]
            + right[job, 1 + start : 1 + stop]
        )

    slots1, slots2 = (left1_s, middle1_s, right1_s), (left2_s, middle2_s, right2_s)

    def behind(start, stop):
        return max(0, start - LAG), (stop if stop == width else stop - LAG)

    def grid(rows):
        return [(f, row) for row in rows for f in range(2)]

    def wait_halo(k):
        @pl.when(has_down)
        def _():
            halo_copy(0, k).wait_recv()

        @pl.when(has_up)
        def _():
            halo_copy(1, k).wait_recv()

    def conv_rows(rows1, rows2, start, stop):
        products(att, grid(rows1), 0, slots1, start, stop)
        start, stop = behind(start, stop)
        for f, row in grid(rows1):
            total = jnp.maximum(summed(slots1, f, row, start, stop), 0.0)
            if row == 0:
                total = jnp.where(has_up, total, 0.0)
            if row == own_rows + 1:
                total = jnp.where(has_down, total, 0.0)
            inner[f, row, start:stop] = total.astype(BF16)
        products(inner, grid(rows2), 1, slots2, start, stop)
        start, stop = behind(start, stop)
        for f, row in grid(rows2):
            total = att[f, row + HALO, start:stop].astype(F32)
            total = total + summed(slots2, f, row, start, stop)
            out_ref[f, row, start:stop] = total[:, :C].astype(BF16)

    def conv_inside(k):
        rows1, rows2 = range(2, own_rows), range(2, own_rows - 2)
        conv_rows(rows1, rows2, spans[k][0] * WIN, spans[k][1] * WIN)

    for k, (first, last) in enumerate(spans):
        if k > 0:
            conv_inside(k - 1)

        @pl.when(has_prev)
        def _(k=k):
            clip_copy(0, k).wait_recv()

        @pl.when(has_next)
        def _(k=k):
            clip_copy(1, k).wait_recv()

        mutual_chunk(first, last)

        @pl.when(has_up)
        def _(k=k):
            halo_copy(0, k).start()

        @pl.when(has_down)
        def _(k=k):
            halo_copy(1, k).start()

    conv_inside(len(spans) - 1)
    for k in range(len(spans)):
        wait_halo(k)
    last_row = own_rows - 1
    conv_rows(
        (0, 1, own_rows, own_rows + 1), (0, 1, last_row - 1, last_row), 0, width
    )

    for k in range(len(spans)):
        for copy, low, high in ((clip_copy, has_next, has_prev), (halo_copy, has_up, has_down)):

            @pl.when(low)
            def _(copy=copy, k=k):
                copy(0, k).wait_send()

            @pl.when(high)
            def _(copy=copy, k=k):
                copy(1, k).wait_send()


def shards(frames, ln_gain, w_qkv, w_proj, conv_weight):
    c, f, h, w = frames.shape
    windows = w // WIN
    clips, parts = lax.axis_size("clip"), lax.axis_size("ha")
    tokens = frames.transpose(1, 2, 3, 0)
    vmem = pl.BlockSpec(memory_space=pltpu.VMEM)
    restored = pl.pallas_call(
        functools.partial(kernel, clips, parts),
        out_shape=jax.ShapeDtypeStruct((f, h, w, c), BF16),
        in_specs=[vmem] * 4 + [pl.BlockSpec(memory_space=pl.ANY)],
        out_specs=vmem,
        scratch_shapes=[
            pltpu.VMEM((windows, TOK, CP), BF16),
            pltpu.VMEM((2, windows, TOK, CP), BF16),
            pltpu.VMEM((windows, CP, TOK), BF16),
            pltpu.VMEM((windows, TOK, CP), BF16),
            pltpu.VMEM((windows, HEADS * DP, TOK), BF16),
            pltpu.VMEM((windows, 2 * TOK, CP), BF16),
            pltpu.VMEM((windows, HEADS * DP, 2 * TOK), BF16),
            pltpu.VMEM((windows, 2 * HEADS * DP, TOK), BF16),
            pltpu.VMEM((f, h + 2 * HALO, w, CP), BF16),
            pltpu.VMEM((f, h + 2, w, CP), BF16),
            pltpu.VMEM((CP, CP), BF16),
            pltpu.VMEM((CP, CP), BF16),
            pltpu.VMEM((HEADS * DP, CP), BF16),
            pltpu.VMEM((CP, 2 * HEADS * DP), BF16),
            pltpu.VMEM((2, 3 * CP, 3 * CP), BF16),
            pltpu.VMEM((HEADS, CP, TOK), BF16),
            *[pltpu.VMEM((f * (h + 2), w + 16, CP), F32) for _ in range(6)],
            pltpu.VMEM(conv_weight.shape, BF16),
            pltpu.SemaphoreType.DMA,
            pltpu.SemaphoreType.DMA((2, len(CUTS))),
            pltpu.SemaphoreType.DMA((2, len(CUTS))),
            pltpu.SemaphoreType.DMA((2, len(CUTS))),
            pltpu.SemaphoreType.DMA((2, len(CUTS))),
        ],
        compiler_params=pltpu.CompilerParams(
            collective_id=0, has_side_effects=True, vmem_limit_bytes=48 * 1024 * 1024
        ),
    )(tokens, ln_gain.reshape(1, c), w_qkv, w_proj, conv_weight)
    return restored.transpose(3, 0, 1, 2)


def solution(mesh):
    return jax.shard_map(
        shards,
        mesh=mesh,
        in_specs=(P(None, "clip", "ha", None), P(), P(), P(), P()),
        out_specs=P(None, "clip", "ha", None),
        check_vma=False,
    )
```

```python
import functools
import math

import jax
import jax.numpy as jnp
from jax import lax
from jax.experimental import pallas as pl
from jax.experimental.pallas import tpu as pltpu
from jax.sharding import PartitionSpec as P

HEADS = 6
WIN = 8
C = 120
D = C // HEADS
CP = 128
DP = 32
TOK = 2 * WIN * WIN
HALO = 2
CUTS = (8, 8, 8, 4, 4)
GROUP = 8
LAG = 16
LAG1 = 4
LAG2 = 6
LAG3 = 8
MESH = pl.DeviceIdType.MESH
F32 = jnp.float32
BF16 = jnp.bfloat16


def dot(a, b):
    return lax.dot_general(a, b, (((1,), (0,)), ((), ())), preferred_element_type=F32)


def dot_nt(a, b):
    return lax.dot_general(a, b, (((1,), (1,)), ((), ())), preferred_element_type=F32)


def iota(shape, dim):
    return lax.broadcasted_iota(jnp.int32, shape, dim)


def one_hot_heads(rows, cols, padded_dim):
    padded = iota((rows, cols), padded_dim)
    packed = iota((rows, cols), 1 - padded_dim)
    entry = padded & (DP - 1)
    hit = ((padded >> 5) * D + entry == packed) & (entry < D)
    return jnp.where(hit, 1.0, 0.0).astype(BF16)


def pad_rows(value, rows):
    extra = jnp.zeros((rows - value.shape[0], value.shape[1]), value.dtype)
    return jnp.concatenate([value, extra], axis=0)


def kernel(
    clips,
    parts,
    x_ref,
    gain_ref,
    wqkv_ref,
    wproj_ref,
    wconv_ref,
    out_ref,
    xn,
    sent,
    xin,
    q_s,
    k_s,
    v_s,
    k2_s,
    v2_s,
    o_s,
    att,
    inner,
    wq_s,
    wk_s,
    wv_s,
    wp_s,
    wc_s,
    mask_s,
    left1_s,
    middle1_s,
    right1_s,
    left2_s,
    middle2_s,
    right2_s,
    send_sem,
    recv_sem,
    hsend_sem,
    hrecv_sem,
):
    me = lax.axis_index("clip")
    ha = lax.axis_index("ha")
    width = x_ref.shape[2]
    windows = width // WIN
    own_rows = x_ref.shape[1]
    spans = []
    for size in CUTS:
        start = sum(CUTS[: len(spans)])
        spans.append((start, start + size))
    has_prev, has_next = me > 0, me < clips - 1
    has_up, has_down = ha > 0, ha < parts - 1

    lane_one = jnp.where(iota((TOK, CP), 1) == C, 1.0, 0.0).astype(BF16)

    barrier = pltpu.get_barrier_semaphore()
    neighbours = (
        (has_prev, (me - 1, ha)),
        (has_next, (me + 1, ha)),
        (has_up, (me, ha - 1)),
        (has_down, (me, ha + 1)),
    )
    for there, device in neighbours:

        @pl.when(there)
        def _(device=device):
            pl.semaphore_signal(barrier, inc=1, device_id=device, device_id_type=MESH)

    gain = gain_ref[...].reshape(1, C)

    def norm_pair(p, carry):
        cols = pl.ds(pl.multiple_of(p * 2 * WIN, 2 * WIN), 2 * WIN)
        x = x_ref[:, :, cols].astype(F32).reshape(2, own_rows, 2, WIN, C)
        x = x.transpose(2, 0, 1, 3, 4).reshape(2, TOK, C)
        centred = x - jnp.mean(x, axis=-1, keepdims=True)
        spread = jnp.mean(centred * centred, axis=-1, keepdims=True)
        normed = centred * lax.rsqrt(spread + 1e-05) * gain
        for i in range(2):
            xn[2 * p + i] = lane_one
        xn[pl.ds(2 * p, 2), :, :C] = normed.astype(BF16)
        packed = jnp.concatenate([normed[0].T, normed[1].T], axis=0)
        sent[pl.ds(pl.multiple_of(p * 2 * C, 2 * C), 2 * C)] = packed.astype(BF16)
        return carry

    def clip_copy(side, k):
        first, last = spans[k]
        part = pl.ds(first * C, (last - first) * C)
        return pltpu.make_async_remote_copy(
            src_ref=sent.at[part],
            dst_ref=xin.at[side, part],
            send_sem=send_sem.at[side, k],
            recv_sem=recv_sem.at[side, k],
            device_id=(me + 1 - 2 * side, ha),
            device_id_type=MESH,
        )

    for k, (first, last) in enumerate(spans):
        lax.fori_loop(first // 2, last // 2, norm_pair, 0, unroll=2)
        if k == 0:
            pl.semaphore_wait(barrier, sum(jnp.where(there, 1, 0) for there, _ in neighbours))

        @pl.when(has_next)
        def _(k=k):
            clip_copy(0, k).start()

        @pl.when(has_prev)
        def _(k=k):
            clip_copy(1, k).start()

    own = slice(HALO, HALO + own_rows)
    att[:, own] = jnp.zeros((2, own_rows, width, CP), BF16)

    @pl.when(jnp.logical_not(has_up))
    def _():
        att[:, :HALO] = jnp.zeros((2, HALO, width, CP), BF16)

    @pl.when(jnp.logical_not(has_down))
    def _():
        att[:, HALO + own_rows :] = jnp.zeros((2, HALO, width, CP), BF16)

    wqkv = wqkv_ref[...].astype(F32)
    for slot, start in ((wq_s, 0), (wk_s, C)):
        slot[...] = jnp.zeros_like(slot)
        slot[:, :C] = pad_rows(wqkv[start : start + C], CP).astype(BF16)
    wv = dot(one_hot_heads(HEADS * DP, C, 0), wqkv[2 * C :].astype(BF16))
    ones_row = (iota((HEADS * DP, CP), 0) & (DP - 1) == D) & (iota((HEADS * DP, CP), 1) == C)
    wv_s[...] = jnp.where(ones_row, 1.0, 0.0).astype(BF16)
    wv_s[:, :C] = wv.astype(BF16)
    wp = dot(wproj_ref[...], one_hot_heads(2 * C, 2 * HEADS * DP, 1))
    wp_s[...] = pad_rows(wp, CP).astype(BF16)
    channel = iota((CP, TOK), 0)
    for h in range(HEADS):
        mask_s[h] = jnp.where((channel >= h * D) & (channel < (h + 1) * D), 1.0, 0.0).astype(BF16)

    scale = math.log2(math.e) / math.sqrt(D)

    def attend(ws, keys, values, first_row):
        jobs = [(w, pair) for w in range(len(ws)) for pair in range(HEADS // 2)]
        qs = [q_s[w] for w in ws]
        scores, weights, gots = {}, {}, {}

        def score(j):
            w, pair = jobs[j]
            queries = jnp.concatenate(
                [qs[w] * mask_s[2 * pair], qs[w] * mask_s[2 * pair + 1]], axis=1
            )
            scores[j] = dot(keys[w], queries)

        def weigh(j):
            got = scores.pop(j)
            peak = jnp.max(got, axis=0, keepdims=True)
            weights[j] = jnp.exp2((got - peak) * scale).astype(BF16)

        def gather(j):
            w, pair = jobs[j]
            gots[j] = dot(values[w][2 * pair * DP : 2 * (pair + 1) * DP], weights.pop(j))

        def store(j):
            w, pair = jobs[j]
            got = gots.pop(j)
            for side in range(2):
                mine = got[side * DP : (side + 1) * DP, side * TOK : (side + 1) * TOK]
                mine = mine * (1.0 / mine[D : D + 1])
                start = first_row + (2 * pair + side) * DP
                o_s[ws[w], start : start + DP] = mine.astype(BF16)

        n = len(jobs)
        for t in range(n + LAG2 + LAG3):
            if t < n:
                score(t)
            if 0 <= t - LAG1 < n:
                weigh(t - LAG1)
            if 0 <= t - LAG2 < n:
                gather(t - LAG2)
            if 0 <= t - LAG3 < n:
                store(t - LAG3)

    def project_own(g, carry):
        ws = pl.ds(g * GROUP, GROUP)
        x = xn[ws].reshape(GROUP * TOK, CP)
        k_s[ws] = dot_nt(x, wk_s[...]).astype(BF16).reshape(GROUP, TOK, CP)
        q = dot_nt(wq_s[...], x).astype(BF16)
        v = dot_nt(wv_s[...], x).astype(BF16)
        for i in range(GROUP):
            q_s[g * GROUP + i] = q[:, i * TOK : (i + 1) * TOK]
            v_s[g * GROUP + i] = v[:, i * TOK : (i + 1) * TOK]
        return carry

    lax.fori_loop(0, windows // GROUP, project_own, 0)

    def self_window(g, carry):
        ws = [g * GROUP + i for i in range(GROUP)]
        attend(ws, [k_s[w] for w in ws], [v_s[w] for w in ws], 0)
        return carry

    lax.fori_loop(0, windows // GROUP, self_window, 0)

    wc_s[...] = jnp.zeros_like(wc_s)
    for layer in range(2):
        for r in range(3):
            for s in range(3):
                weight = pad_rows(wconv_ref[layer, r, s].astype(F32), CP).astype(BF16)
                wc_s[layer, s * CP : (s + 1) * CP, r * CP : r * CP + C] = weight
    for slot, row in ((left1_s, 0), (left2_s, 0), (right1_s, width), (right2_s, width)):
        slot[:, row : row + 8] = jnp.zeros((slot.shape[0], 8, CP), F32)

    slot_prev = jnp.where(has_prev, 0, 1)
    slot_next = jnp.where(has_next, 1, 0)

    top = jnp.where(iota((CP - C, TOK), 0) == 0, 1.0, 0.0)

    def mutual_chunk(first, last):
        ws = pl.ds(first, last - first)
        for side, slot in ((0, slot_prev), (1, slot_next)):
            x = []
            for w in range(first, last, 2):
                both = xin[slot, w * C : (w + 2) * C].astype(F32)
                for i in range(2):
                    x.append(jnp.concatenate([both[i * C : (i + 1) * C], top], axis=0).T)
            x = jnp.concatenate(x, axis=0).astype(BF16)
            part = slice(side * TOK, (side + 1) * TOK)
            k2_s[ws, part] = dot_nt(x, wk_s[...]).astype(BF16).reshape(last - first, TOK, CP)
            v = dot_nt(wv_s[...], x).astype(BF16)
            for i in range(last - first):
                v2_s[first + i, :, part] = v[:, i * TOK : (i + 1) * TOK]
        every = list(range(first, last))
        attend(every, [k2_s[w] for w in every], [v2_s[w] for w in every], HEADS * DP)
        mixed = [dot(wp_s[...], o_s[w]) for w in every]
        mixed = [m.T[:, :C] for m in mixed]
        for i in range(0, len(every), 2):
            shaped = jnp.stack(mixed[i : i + 2], axis=0).reshape(2, 2, own_rows, WIN, C)
            shaped = shaped.transpose(1, 2, 0, 3, 4).reshape(2, own_rows, 2 * WIN, C)
            cols = slice(every[i] * WIN, every[i] * WIN + 2 * WIN)
            total = x_ref[:, :, cols].astype(F32) + shaped
            att[:, HALO : HALO + own_rows, cols, :C] = total.astype(BF16)

    def halo_copy(side, k):
        first, last = spans[k]
        cols = pl.ds(first * WIN, (last - first) * WIN)
        src_row = own_rows if side else HALO
        dst_row = 0 if side else HALO + own_rows
        return pltpu.make_async_remote_copy(
            src_ref=att.at[:, pl.ds(src_row, HALO), cols],
            dst_ref=att.at[:, pl.ds(dst_row, HALO), cols],
            send_sem=hsend_sem.at[side, k],
            recv_sem=hrecv_sem.at[side, k],
            device_id=(me, ha + (1 if side else -1)),
            device_id_type=MESH,
        )

    def products(field, jobs, layer, slots, start, stop):
        stacked = jnp.concatenate(
            [
                jnp.concatenate([field[f, row + r, start:stop] for r in range(3)], axis=1)
                for f, row in jobs
            ],
            axis=0,
        )
        part = dot_nt(stacked, wc_s[layer])
        size = stop - start
        left, middle, right = slots
        for i, (f, row) in enumerate(jobs):
            job = f * (own_rows + 2) + row
            mine = part[i * size : (i + 1) * size]
            left[job, 8 + start : 8 + stop] = mine[:, :CP]
            middle[job, start:stop] = mine[:, CP : 2 * CP]
            right[job, start:stop] = mine[:, 2 * CP :]

    def summed(slots, f, row, start, stop):
        left, middle, right = slots
        job = f * (own_rows + 2) + row
        return (
            middle[job, start:stop]
            + left[job, 7 + start : 7 + stop]
            + right[job, 1 + start : 1 + stop]
        )

    slots1, slots2 = (left1_s, middle1_s, right1_s), (left2_s, middle2_s, right2_s)

    def behind(start, stop):
        return max(0, start - LAG), (stop if stop == width else stop - LAG)

    def grid(rows):
        return [(f, row) for row in rows for f in range(2)]

    def wait_halo(k):
        @pl.when(has_down)
        def _():
            halo_copy(0, k).wait_recv()

        @pl.when(has_up)
        def _():
            halo_copy(1, k).wait_recv()

    def conv_rows(rows1, rows2, start, stop):
        products(att, grid(rows1), 0, slots1, start, stop)
        start, stop = behind(start, stop)
        for f, row in grid(rows1):
            total = jnp.maximum(summed(slots1, f, row, start, stop), 0.0)
            if row == 0:
                total = jnp.where(has_up, total, 0.0)
            if row == own_rows + 1:
                total = jnp.where(has_down, total, 0.0)
            inner[f, row, start:stop] = total.astype(BF16)
        products(inner, grid(rows2), 1, slots2, start, stop)
        start, stop = behind(start, stop)
        for f, row in grid(rows2):
            total = att[f, row + HALO, start:stop].astype(F32)
            total = total + summed(slots2, f, row, start, stop)
            out_ref[f, row, start:stop] = total[:, :C].astype(BF16)

    def conv_inside(start, stop):
        conv_rows(range(2, own_rows), range(2, own_rows - 2), start, stop)

    done = 0
    for k, (first, last) in enumerate(spans):
        if k > 1:
            conv_inside(done, first * WIN)
            done = first * WIN

        @pl.when(has_prev)
        def _(k=k):
            clip_copy(0, k).wait_recv()

        @pl.when(has_next)
        def _(k=k):
            clip_copy(1, k).wait_recv()

        mutual_chunk(first, last)

        @pl.when(has_up)
        def _(k=k):
            halo_copy(0, k).start()

        @pl.when(has_down)
        def _(k=k):
            halo_copy(1, k).start()

    conv_inside(done, width)
    rows1 = (0, 1, own_rows, own_rows + 1)
    rows2 = (0, 1, own_rows - 2, own_rows - 1)
    for k in range(len(spans) - 1):
        wait_halo(k)
    conv_rows(rows1, rows2, 0, spans[-1][0] * WIN)
    wait_halo(len(spans) - 1)
    conv_rows(rows1, rows2, spans[-1][0] * WIN, width)

    for k in range(len(spans)):
        for copy, low, high in ((clip_copy, has_next, has_prev), (halo_copy, has_up, has_down)):

            @pl.when(low)
            def _(copy=copy, k=k):
                copy(0, k).wait_send()

            @pl.when(high)
            def _(copy=copy, k=k):
                copy(1, k).wait_send()


def shards(frames, ln_gain, w_qkv, w_proj, conv_weight):
    c, f, h, w = frames.shape
    windows = w // WIN
    clips, parts = lax.axis_size("clip"), lax.axis_size("ha")
    tokens = frames.transpose(1, 2, 3, 0)
    vmem = pl.BlockSpec(memory_space=pltpu.VMEM)
    restored = pl.pallas_call(
        functools.partial(kernel, clips, parts),
        out_shape=jax.ShapeDtypeStruct((f, h, w, c), BF16),
        in_specs=[vmem] * 5,
        out_specs=vmem,
        scratch_shapes=[
            pltpu.VMEM((windows, TOK, CP), BF16),
            pltpu.VMEM((windows * c, TOK), BF16),
            pltpu.VMEM((2, windows * c, TOK), BF16),
            pltpu.VMEM((windows, CP, TOK), BF16),
            pltpu.VMEM((windows, TOK, CP), BF16),
            pltpu.VMEM((windows, HEADS * DP, TOK), BF16),
            pltpu.VMEM((windows, 2 * TOK, CP), BF16),
            pltpu.VMEM((windows, HEADS * DP, 2 * TOK), BF16),
            pltpu.VMEM((windows, 2 * HEADS * DP, TOK), BF16),
            pltpu.VMEM((f, h + 2 * HALO, w, CP), BF16),
            pltpu.VMEM((f, h + 2, w, CP), BF16),
            pltpu.VMEM((CP, CP), BF16),
            pltpu.VMEM((CP, CP), BF16),
            pltpu.VMEM((HEADS * DP, CP), BF16),
            pltpu.VMEM((CP, 2 * HEADS * DP), BF16),
            pltpu.VMEM((2, 3 * CP, 3 * CP), BF16),
            pltpu.VMEM((HEADS, CP, TOK), BF16),
            *[pltpu.VMEM((f * (h + 2), w + 16, CP), F32) for _ in range(6)],
            pltpu.SemaphoreType.DMA((2, len(CUTS))),
            pltpu.SemaphoreType.DMA((2, len(CUTS))),
            pltpu.SemaphoreType.DMA((2, len(CUTS))),
            pltpu.SemaphoreType.DMA((2, len(CUTS))),
        ],
        compiler_params=pltpu.CompilerParams(
            collective_id=0, has_side_effects=True, vmem_limit_bytes=48 * 1024 * 1024
        ),
    )(tokens, ln_gain, w_qkv, w_proj, conv_weight)
    return restored.transpose(3, 0, 1, 2)


def solution(mesh):
    return jax.shard_map(
        shards,
        mesh=mesh,
        in_specs=(P(None, "clip", "ha", None), P(), P(), P(), P()),
        out_specs=P(None, "clip", "ha", None),
        check_vma=False,
    )
```

```python
import functools
import math

import jax
import jax.numpy as jnp
from jax import lax
from jax.experimental import pallas as pl
from jax.experimental.pallas import tpu as pltpu
from jax.sharding import PartitionSpec as P

HEADS = 6
WIN = 8
C = 120
D = C // HEADS
CP = 128
DP = 32
TOK = 2 * WIN * WIN
HALO = 2
CUTS = (8, 8, 8, 4, 4)
GROUP = 8
LAG = 16
LAG1 = 4
LAG2 = 6
LAG3 = 8
MESH = pl.DeviceIdType.MESH
F32 = jnp.float32
BF16 = jnp.bfloat16


def dot(a, b):
    return lax.dot_general(a, b, (((1,), (0,)), ((), ())), preferred_element_type=F32)


def dot_nt(a, b):
    return lax.dot_general(a, b, (((1,), (1,)), ((), ())), preferred_element_type=F32)


def iota(shape, dim):
    return lax.broadcasted_iota(jnp.int32, shape, dim)


def one_hot_heads(rows, cols, padded_dim):
    padded = iota((rows, cols), padded_dim)
    packed = iota((rows, cols), 1 - padded_dim)
    entry = padded & (DP - 1)
    hit = ((padded >> 5) * D + entry == packed) & (entry < D)
    return jnp.where(hit, 1.0, 0.0).astype(BF16)


def pad_rows(value, rows):
    extra = jnp.zeros((rows - value.shape[0], value.shape[1]), value.dtype)
    return jnp.concatenate([value, extra], axis=0)


def kernel(
    clips,
    parts,
    x_ref,
    gain_ref,
    wqkv_ref,
    wproj_ref,
    wconv_ref,
    out_ref,
    xn,
    sent,
    xin,
    q_s,
    k_s,
    v_s,
    k2_s,
    v2_s,
    o_s,
    att,
    inner,
    wq_s,
    wk_s,
    wv_s,
    wp_s,
    wc_s,
    mask_s,
    left1_s,
    middle1_s,
    right1_s,
    left2_s,
    middle2_s,
    right2_s,
    send_sem,
    recv_sem,
    hsend_sem,
    hrecv_sem,
):
    me = lax.axis_index("clip")
    ha = lax.axis_index("ha")
    width = x_ref.shape[2]
    windows = width // WIN
    own_rows = x_ref.shape[1]
    spans = []
    for size in CUTS:
        start = sum(CUTS[: len(spans)])
        spans.append((start, start + size))
    has_prev, has_next = me > 0, me < clips - 1
    has_up, has_down = ha > 0, ha < parts - 1

    lane_one = jnp.where(iota((TOK, CP), 1) == C, 1.0, 0.0).astype(BF16)

    barrier = pltpu.get_barrier_semaphore()
    neighbours = (
        (has_prev, (me - 1, ha)),
        (has_next, (me + 1, ha)),
        (has_up, (me, ha - 1)),
        (has_down, (me, ha + 1)),
    )
    for there, device in neighbours:

        @pl.when(there)
        def _(device=device):
            pl.semaphore_signal(barrier, inc=1, device_id=device, device_id_type=MESH)

    gain = gain_ref[...].reshape(1, C)

    def norm_pair(p, carry):
        cols = pl.ds(pl.multiple_of(p * 2 * WIN, 2 * WIN), 2 * WIN)
        x = x_ref[:, :, cols].astype(F32).reshape(2, own_rows, 2, WIN, C)
        x = x.transpose(2, 0, 1, 3, 4).reshape(2, TOK, C)
        centred = x - jnp.mean(x, axis=-1, keepdims=True)
        spread = jnp.mean(centred * centred, axis=-1, keepdims=True)
        normed = centred * lax.rsqrt(spread + 1e-05) * gain
        for i in range(2):
            xn[2 * p + i] = lane_one
        xn[pl.ds(2 * p, 2), :, :C] = normed.astype(BF16)
        packed = jnp.concatenate([normed[0].T, normed[1].T], axis=0)
        sent[pl.ds(pl.multiple_of(p * 2 * C, 2 * C), 2 * C)] = packed.astype(BF16)
        return carry

    def clip_copy(side, k):
        first, last = spans[k]
        part = pl.ds(first * C, (last - first) * C)
        return pltpu.make_async_remote_copy(
            src_ref=sent.at[part],
            dst_ref=xin.at[side, part],
            send_sem=send_sem.at[side, k],
            recv_sem=recv_sem.at[side, k],
            device_id=(me + 1 - 2 * side, ha),
            device_id_type=MESH,
        )

    for k, (first, last) in enumerate(spans):
        lax.fori_loop(first // 2, last // 2, norm_pair, 0, unroll=2)
        if k == 0:
            pl.semaphore_wait(barrier, sum(jnp.where(there, 1, 0) for there, _ in neighbours))

        @pl.when(has_next)
        def _(k=k):
            clip_copy(0, k).start()

        @pl.when(has_prev)
        def _(k=k):
            clip_copy(1, k).start()

    own = slice(HALO, HALO + own_rows)
    att[:, own] = jnp.zeros((2, own_rows, width, CP), BF16)

    @pl.when(jnp.logical_not(has_up))
    def _():
        att[:, :HALO] = jnp.zeros((2, HALO, width, CP), BF16)

    @pl.when(jnp.logical_not(has_down))
    def _():
        att[:, HALO + own_rows :] = jnp.zeros((2, HALO, width, CP), BF16)

    wqkv = wqkv_ref[...].astype(F32)
    for slot, start in ((wq_s, 0), (wk_s, C)):
        slot[...] = jnp.zeros_like(slot)
        slot[:, :C] = pad_rows(wqkv[start : start + C], CP).astype(BF16)
    wv = dot(one_hot_heads(HEADS * DP, C, 0), wqkv[2 * C :].astype(BF16))
    ones_row = (iota((HEADS * DP, CP), 0) & (DP - 1) == D) & (iota((HEADS * DP, CP), 1) == C)
    wv_s[...] = jnp.where(ones_row, 1.0, 0.0).astype(BF16)
    wv_s[:, :C] = wv.astype(BF16)
    wp = dot(wproj_ref[...], one_hot_heads(2 * C, 2 * HEADS * DP, 1))
    wp_s[...] = pad_rows(wp, CP).astype(BF16)
    channel = iota((CP, TOK), 0)
    for h in range(HEADS):
        mask_s[h] = jnp.where((channel >= h * D) & (channel < (h + 1) * D), 1.0, 0.0).astype(BF16)

    scale = math.log2(math.e) / math.sqrt(D)

    def attend(ws, keys, values, first_row):
        jobs = [(w, pair) for w in range(len(ws)) for pair in range(HEADS // 2)]
        qs = [q_s[w] for w in ws]
        scores, weights, gots = {}, {}, {}

        def score(j):
            w, pair = jobs[j]
            queries = jnp.concatenate(
                [qs[w] * mask_s[2 * pair], qs[w] * mask_s[2 * pair + 1]], axis=1
            )
            scores[j] = dot(keys[w], queries)

        def weigh(j):
            got = scores.pop(j)
            peak = jnp.max(got, axis=0, keepdims=True)
            weights[j] = jnp.exp2((got - peak) * scale).astype(BF16)

        def gather(j):
            w, pair = jobs[j]
            gots[j] = dot(values[w][2 * pair * DP : 2 * (pair + 1) * DP], weights.pop(j))

        def store(j):
            w, pair = jobs[j]
            got = gots.pop(j)
            for side in range(2):
                mine = got[side * DP : (side + 1) * DP, side * TOK : (side + 1) * TOK]
                mine = mine * (1.0 / mine[D : D + 1])
                start = first_row + (2 * pair + side) * DP
                o_s[ws[w], start : start + DP] = mine.astype(BF16)

        n = len(jobs)
        for t in range(n + LAG2 + LAG3):
            if t < n:
                score(t)
            if 0 <= t - LAG1 < n:
                weigh(t - LAG1)
            if 0 <= t - LAG2 < n:
                gather(t - LAG2)
            if 0 <= t - LAG3 < n:
                store(t - LAG3)

    def project_own(g, carry):
        ws = pl.ds(g * GROUP, GROUP)
        x = xn[ws].reshape(GROUP * TOK, CP)
        k_s[ws] = dot_nt(x, wk_s[...]).astype(BF16).reshape(GROUP, TOK, CP)
        q = dot_nt(wq_s[...], x).astype(BF16)
        v = dot_nt(wv_s[...], x).astype(BF16)
        for i in range(GROUP):
            q_s[g * GROUP + i] = q[:, i * TOK : (i + 1) * TOK]
            v_s[g * GROUP + i] = v[:, i * TOK : (i + 1) * TOK]
        return carry

    lax.fori_loop(0, windows // GROUP, project_own, 0)

    def self_window(g, carry):
        ws = [g * GROUP + i for i in range(GROUP)]
        attend(ws, [k_s[w] for w in ws], [v_s[w] for w in ws], 0)
        return carry

    lax.fori_loop(0, windows // GROUP, self_window, 0)

    for layer in range(2):
        for r in range(3):
            for s in range(3):
                weight = pad_rows(wconv_ref[layer, r, s].astype(F32), CP).T
                weight = pad_rows(weight, CP).astype(BF16)
                wc_s[layer, r * CP : (r + 1) * CP, s * CP : (s + 1) * CP] = weight
    for slot, row in ((left1_s, 0), (left2_s, 0), (right1_s, width), (right2_s, width)):
        slot[:, row : row + 8] = jnp.zeros((slot.shape[0], 8, CP), F32)

    slot_prev = jnp.where(has_prev, 0, 1)
    slot_next = jnp.where(has_next, 1, 0)

    top = jnp.where(iota((CP - C, TOK), 0) == 0, 1.0, 0.0)

    def mutual_chunk(first, last):
        ws = pl.ds(first, last - first)
        for side, slot in ((0, slot_prev), (1, slot_next)):
            x = []
            for w in range(first, last, 2):
                both = xin[slot, w * C : (w + 2) * C].astype(F32)
                for i in range(2):
                    x.append(jnp.concatenate([both[i * C : (i + 1) * C], top], axis=0).T)
            x = jnp.concatenate(x, axis=0).astype(BF16)
            part = slice(side * TOK, (side + 1) * TOK)
            k2_s[ws, part] = dot_nt(x, wk_s[...]).astype(BF16).reshape(last - first, TOK, CP)
            v = dot_nt(wv_s[...], x).astype(BF16)
            for i in range(last - first):
                v2_s[first + i, :, part] = v[:, i * TOK : (i + 1) * TOK]
        every = list(range(first, last))
        attend(every, [k2_s[w] for w in every], [v2_s[w] for w in every], HEADS * DP)
        mixed = [dot(wp_s[...], o_s[w]) for w in every]
        mixed = [m.T[:, :C] for m in mixed]
        for i in range(0, len(every), 2):
            shaped = jnp.stack(mixed[i : i + 2], axis=0).reshape(2, 2, own_rows, WIN, C)
            shaped = shaped.transpose(1, 2, 0, 3, 4).reshape(2, own_rows, 2 * WIN, C)
            cols = slice(every[i] * WIN, every[i] * WIN + 2 * WIN)
            total = x_ref[:, :, cols].astype(F32) + shaped
            att[:, HALO : HALO + own_rows, cols, :C] = total.astype(BF16)

    def halo_copy(side, k):
        first, last = spans[k]
        cols = pl.ds(first * WIN, (last - first) * WIN)
        src_row = own_rows if side else HALO
        dst_row = 0 if side else HALO + own_rows
        return pltpu.make_async_remote_copy(
            src_ref=att.at[:, pl.ds(src_row, HALO), cols],
            dst_ref=att.at[:, pl.ds(dst_row, HALO), cols],
            send_sem=hsend_sem.at[side, k],
            recv_sem=hrecv_sem.at[side, k],
            device_id=(me, ha + (1 if side else -1)),
            device_id_type=MESH,
        )

    def products(field, every, layer, slots, start, stop):
        for first in range(0, len(every), 4):
            product(field, every[first : first + 4], layer, slots, start, stop)

    def product(field, jobs, layer, slots, start, stop):
        stacked = jnp.concatenate(
            [
                jnp.concatenate([field[f, row + r, start:stop] for r in range(3)], axis=1)
                for f, row in jobs
            ],
            axis=0,
        )
        part = dot(stacked, wc_s[layer])
        size = stop - start
        left, middle, right = slots
        for i, (f, row) in enumerate(jobs):
            job = f * (own_rows + 2) + row
            mine = part[i * size : (i + 1) * size]
            left[job, 8 + start : 8 + stop] = mine[:, :CP]
            middle[job, start:stop] = mine[:, CP : 2 * CP]
            right[job, start:stop] = mine[:, 2 * CP :]

    def summed(slots, f, row, start, stop):
        left, middle, right = slots
        job = f * (own_rows + 2) + row
        return (
            middle[job, start:stop]
            + left[job, 7 + start : 7 + stop]
            + right[job, 1 + start : 1 + stop]
        )

    slots1, slots2 = (left1_s, middle1_s, right1_s), (left2_s, middle2_s, right2_s)

    def behind(start, stop):
        return max(0, start - LAG), (stop if stop == width else stop - LAG)

    def grid(rows):
        return [(f, row) for row in rows for f in range(2)]

    def wait_halo(k):
        @pl.when(has_down)
        def _():
            halo_copy(0, k).wait_recv()

        @pl.when(has_up)
        def _():
            halo_copy(1, k).wait_recv()

    def conv_rows(rows1, rows2, start, stop):
        products(att, grid(rows1), 0, slots1, start, stop)
        start, stop = behind(start, stop)
        for f, row in grid(rows1):
            total = jnp.maximum(summed(slots1, f, row, start, stop), 0.0)
            if row == 0:
                total = jnp.where(has_up, total, 0.0)
            if row == own_rows + 1:
                total = jnp.where(has_down, total, 0.0)
            inner[f, row, start:stop] = total.astype(BF16)
        products(inner, grid(rows2), 1, slots2, start, stop)
        start, stop = behind(start, stop)
        for f, row in grid(rows2):
            total = att[f, row + HALO, start:stop].astype(F32)
            total = total + summed(slots2, f, row, start, stop)
            out_ref[f, row, start:stop] = total[:, :C].astype(BF16)

    def conv_inside(start, stop):
        conv_rows(range(2, own_rows), range(2, own_rows - 2), start, stop)

    done = 0
    for k, (first, last) in enumerate(spans):
        if k > 1:
            conv_inside(done, first * WIN)
            done = first * WIN

        @pl.when(has_prev)
        def _(k=k):
            clip_copy(0, k).wait_recv()

        @pl.when(has_next)
        def _(k=k):
            clip_copy(1, k).wait_recv()

        mutual_chunk(first, last)

        @pl.when(has_up)
        def _(k=k):
            halo_copy(0, k).start()

        @pl.when(has_down)
        def _(k=k):
            halo_copy(1, k).start()

    conv_inside(done, width)
    rows1 = (0, 1, own_rows, own_rows + 1)
    rows2 = (0, 1, own_rows - 2, own_rows - 1)
    for k in range(len(spans) - 1):
        wait_halo(k)
    conv_rows(rows1, rows2, 0, spans[-1][0] * WIN)
    wait_halo(len(spans) - 1)
    conv_rows(rows1, rows2, spans[-1][0] * WIN, width)

    for k in range(len(spans)):
        for copy, low, high in ((clip_copy, has_next, has_prev), (halo_copy, has_up, has_down)):

            @pl.when(low)
            def _(copy=copy, k=k):
                copy(0, k).wait_send()

            @pl.when(high)
            def _(copy=copy, k=k):
                copy(1, k).wait_send()


def shards(frames, ln_gain, w_qkv, w_proj, conv_weight):
    c, f, h, w = frames.shape
    windows = w // WIN
    clips, parts = lax.axis_size("clip"), lax.axis_size("ha")
    tokens = frames.transpose(1, 2, 3, 0)
    vmem = pl.BlockSpec(memory_space=pltpu.VMEM)
    restored = pl.pallas_call(
        functools.partial(kernel, clips, parts),
        out_shape=jax.ShapeDtypeStruct((f, h, w, c), BF16),
        in_specs=[vmem] * 5,
        out_specs=vmem,
        scratch_shapes=[
            pltpu.VMEM((windows, TOK, CP), BF16),
            pltpu.VMEM((windows * c, TOK), BF16),
            pltpu.VMEM((2, windows * c, TOK), BF16),
            pltpu.VMEM((windows, CP, TOK), BF16),
            pltpu.VMEM((windows, TOK, CP), BF16),
            pltpu.VMEM((windows, HEADS * DP, TOK), BF16),
            pltpu.VMEM((windows, 2 * TOK, CP), BF16),
            pltpu.VMEM((windows, HEADS * DP, 2 * TOK), BF16),
            pltpu.VMEM((windows, 2 * HEADS * DP, TOK), BF16),
            pltpu.VMEM((f, h + 2 * HALO, w, CP), BF16),
            pltpu.VMEM((f, h + 2, w, CP), BF16),
            pltpu.VMEM((CP, CP), BF16),
            pltpu.VMEM((CP, CP), BF16),
            pltpu.VMEM((HEADS * DP, CP), BF16),
            pltpu.VMEM((CP, 2 * HEADS * DP), BF16),
            pltpu.VMEM((2, 3 * CP, 3 * CP), BF16),
            pltpu.VMEM((HEADS, CP, TOK), BF16),
            *[pltpu.VMEM((f * (h + 2), w + 16, CP), F32) for _ in range(6)],
            pltpu.SemaphoreType.DMA((2, len(CUTS))),
            pltpu.SemaphoreType.DMA((2, len(CUTS))),
            pltpu.SemaphoreType.DMA((2, len(CUTS))),
            pltpu.SemaphoreType.DMA((2, len(CUTS))),
        ],
        compiler_params=pltpu.CompilerParams(
            collective_id=0, has_side_effects=True, vmem_limit_bytes=48 * 1024 * 1024
        ),
    )(tokens, ln_gain, w_qkv, w_proj, conv_weight)
    return restored.transpose(3, 0, 1, 2)


def solution(mesh):
    return jax.shard_map(
        shards,
        mesh=mesh,
        in_specs=(P(None, "clip", "ha", None), P(), P(), P(), P()),
        out_specs=P(None, "clip", "ha", None),
        check_vma=False,
    )
```

```python
import functools
import math

import jax
import jax.numpy as jnp
from jax import lax
from jax.experimental import pallas as pl
from jax.experimental.pallas import tpu as pltpu
from jax.sharding import PartitionSpec as P

HEADS = 6
WIN = 8
C = 120
D = C // HEADS
CP = 128
DP = 32
TOK = 2 * WIN * WIN
HALO = 2
CUTS = (8, 8, 8, 4, 4)
GROUP = 8
LAG = 16
LAG1 = 6
LAG2 = 8
LAG3 = 10
MESH = pl.DeviceIdType.MESH
F32 = jnp.float32
BF16 = jnp.bfloat16


def dot(a, b):
    return lax.dot_general(a, b, (((1,), (0,)), ((), ())), preferred_element_type=F32)


def dot_nt(a, b):
    return lax.dot_general(a, b, (((1,), (1,)), ((), ())), preferred_element_type=F32)


def iota(shape, dim):
    return lax.broadcasted_iota(jnp.int32, shape, dim)


def one_hot_heads(rows, cols, padded_dim):
    padded = iota((rows, cols), padded_dim)
    packed = iota((rows, cols), 1 - padded_dim)
    entry = padded & (DP - 1)
    hit = ((padded >> 5) * D + entry == packed) & (entry < D)
    return jnp.where(hit, 1.0, 0.0).astype(BF16)


def pad_rows(value, rows):
    extra = jnp.zeros((rows - value.shape[0], value.shape[1]), value.dtype)
    return jnp.concatenate([value, extra], axis=0)


def kernel(
    clips,
    parts,
    x_ref,
    gain_ref,
    wqkv_ref,
    wproj_ref,
    wconv_ref,
    out_ref,
    xn,
    sent,
    xin,
    q_s,
    k_s,
    v_s,
    k2_s,
    v2_s,
    o_s,
    att,
    inner,
    wq_s,
    wk_s,
    wv_s,
    wp_s,
    wc_s,
    mask_s,
    left1_s,
    middle1_s,
    right1_s,
    left2_s,
    middle2_s,
    right2_s,
    send_sem,
    recv_sem,
    hsend_sem,
    hrecv_sem,
):
    me = lax.axis_index("clip")
    ha = lax.axis_index("ha")
    width = x_ref.shape[2]
    windows = width // WIN
    own_rows = x_ref.shape[1]
    spans = []
    for size in CUTS:
        start = sum(CUTS[: len(spans)])
        spans.append((start, start + size))
    has_prev, has_next = me > 0, me < clips - 1
    has_up, has_down = ha > 0, ha < parts - 1

    lane_one = jnp.where(iota((TOK, CP), 1) == C, 1.0, 0.0).astype(BF16)

    barrier = pltpu.get_barrier_semaphore()
    neighbours = (
        (has_prev, (me - 1, ha)),
        (has_next, (me + 1, ha)),
        (has_up, (me, ha - 1)),
        (has_down, (me, ha + 1)),
    )
    for there, device in neighbours:

        @pl.when(there)
        def _(device=device):
            pl.semaphore_signal(barrier, inc=1, device_id=device, device_id_type=MESH)

    gain = gain_ref[...].reshape(1, C)

    def norm_pair(p, carry):
        cols = pl.ds(pl.multiple_of(p * 2 * WIN, 2 * WIN), 2 * WIN)
        x = x_ref[:, :, cols].astype(F32).reshape(2, own_rows, 2, WIN, C)
        x = x.transpose(2, 0, 1, 3, 4).reshape(2, TOK, C)
        centred = x - jnp.mean(x, axis=-1, keepdims=True)
        spread = jnp.mean(centred * centred, axis=-1, keepdims=True)
        normed = centred * lax.rsqrt(spread + 1e-05) * gain
        for i in range(2):
            xn[2 * p + i] = lane_one
        xn[pl.ds(2 * p, 2), :, :C] = normed.astype(BF16)
        packed = jnp.concatenate([normed[0].T, normed[1].T], axis=0)
        sent[pl.ds(pl.multiple_of(p * 2 * C, 2 * C), 2 * C)] = packed.astype(BF16)
        return carry

    def clip_copy(side, k):
        first, last = spans[k]
        part = pl.ds(first * C, (last - first) * C)
        return pltpu.make_async_remote_copy(
            src_ref=sent.at[part],
            dst_ref=xin.at[side, part],
            send_sem=send_sem.at[side, k],
            recv_sem=recv_sem.at[side, k],
            device_id=(me + 1 - 2 * side, ha),
            device_id_type=MESH,
        )

    for k, (first, last) in enumerate(spans):
        lax.fori_loop(first // 2, last // 2, norm_pair, 0, unroll=2)
        if k == 0:
            pl.semaphore_wait(barrier, sum(jnp.where(there, 1, 0) for there, _ in neighbours))

        @pl.when(has_next)
        def _(k=k):
            clip_copy(0, k).start()

        @pl.when(has_prev)
        def _(k=k):
            clip_copy(1, k).start()

    own = slice(HALO, HALO + own_rows)
    att[:, own] = jnp.zeros((2, own_rows, width, CP), BF16)

    @pl.when(jnp.logical_not(has_up))
    def _():
        att[:, :HALO] = jnp.zeros((2, HALO, width, CP), BF16)

    @pl.when(jnp.logical_not(has_down))
    def _():
        att[:, HALO + own_rows :] = jnp.zeros((2, HALO, width, CP), BF16)

    wqkv = wqkv_ref[...].astype(F32)
    for slot, start in ((wq_s, 0), (wk_s, C)):
        slot[...] = jnp.zeros_like(slot)
        slot[:, :C] = pad_rows(wqkv[start : start + C], CP).astype(BF16)
    wv = dot(one_hot_heads(HEADS * DP, C, 0), wqkv[2 * C :].astype(BF16))
    ones_row = (iota((HEADS * DP, CP), 0) & (DP - 1) == D) & (iota((HEADS * DP, CP), 1) == C)
    wv_s[...] = jnp.where(ones_row, 1.0, 0.0).astype(BF16)
    wv_s[:, :C] = wv.astype(BF16)
    wp = dot(wproj_ref[...], one_hot_heads(2 * C, 2 * HEADS * DP, 1))
    wp_s[...] = pad_rows(wp, CP).astype(BF16)
    channel = iota((CP, TOK), 0)
    for h in range(HEADS):
        mask_s[h] = jnp.where((channel >= h * D) & (channel < (h + 1) * D), 1.0, 0.0).astype(BF16)

    scale = math.log2(math.e) / math.sqrt(D)

    def attend(ws, keys, values, first_row):
        jobs = [(w, pair) for w in range(len(ws)) for pair in range(HEADS // 2)]
        qs = [q_s[w] for w in ws]
        scores, weights, gots = {}, {}, {}

        def score(j):
            w, pair = jobs[j]
            queries = jnp.concatenate(
                [qs[w] * mask_s[2 * pair], qs[w] * mask_s[2 * pair + 1]], axis=1
            )
            scores[j] = dot(keys[w], queries)

        def weigh(j):
            got = scores.pop(j)
            peak = jnp.max(got, axis=0, keepdims=True)
            weights[j] = jnp.exp2((got - peak) * scale).astype(BF16)

        def gather(j):
            w, pair = jobs[j]
            gots[j] = dot(values[w][2 * pair * DP : 2 * (pair + 1) * DP], weights.pop(j))

        def store(j):
            w, pair = jobs[j]
            got = gots.pop(j)
            for side in range(2):
                mine = got[side * DP : (side + 1) * DP, side * TOK : (side + 1) * TOK]
                mine = mine * (1.0 / mine[D : D + 1])
                start = first_row + (2 * pair + side) * DP
                o_s[ws[w], start : start + DP] = mine.astype(BF16)

        n = len(jobs)
        for t in range(n + LAG2 + LAG3):
            if t < n:
                score(t)
            if 0 <= t - LAG1 < n:
                weigh(t - LAG1)
            if 0 <= t - LAG2 < n:
                gather(t - LAG2)
            if 0 <= t - LAG3 < n:
                store(t - LAG3)

    def project_own(g, carry):
        ws = pl.ds(g * GROUP, GROUP)
        x = xn[ws].reshape(GROUP * TOK, CP)
        k_s[ws] = dot_nt(x, wk_s[...]).astype(BF16).reshape(GROUP, TOK, CP)
        q = dot_nt(wq_s[...], x).astype(BF16)
        v = dot_nt(wv_s[...], x).astype(BF16)
        for i in range(GROUP):
            q_s[g * GROUP + i] = q[:, i * TOK : (i + 1) * TOK]
            v_s[g * GROUP + i] = v[:, i * TOK : (i + 1) * TOK]
        return carry

    lax.fori_loop(0, windows // GROUP, project_own, 0)

    def self_window(g, carry):
        ws = [g * GROUP + i for i in range(GROUP)]
        attend(ws, [k_s[w] for w in ws], [v_s[w] for w in ws], 0)
        return carry

    lax.fori_loop(0, windows // GROUP, self_window, 0)

    for layer in range(2):
        for r in range(3):
            for s in range(3):
                weight = pad_rows(wconv_ref[layer, r, s].astype(F32), CP).T
                weight = pad_rows(weight, CP).astype(BF16)
                wc_s[layer, r * CP : (r + 1) * CP, s * CP : (s + 1) * CP] = weight
    for slot, row in ((left1_s, 0), (left2_s, 0), (right1_s, width), (right2_s, width)):
        slot[:, row : row + 8] = jnp.zeros((slot.shape[0], 8, CP), F32)

    slot_prev = jnp.where(has_prev, 0, 1)
    slot_next = jnp.where(has_next, 1, 0)

    top = jnp.where(iota((CP - C, TOK), 0) == 0, 1.0, 0.0)

    def mutual_chunk(first, last):
        ws = pl.ds(first, last - first)
        for side, slot in ((0, slot_prev), (1, slot_next)):
            x = []
            for w in range(first, last, 2):
                both = xin[slot, w * C : (w + 2) * C].astype(F32)
                for i in range(2):
                    x.append(jnp.concatenate([both[i * C : (i + 1) * C], top], axis=0).T)
            x = jnp.concatenate(x, axis=0).astype(BF16)
            part = slice(side * TOK, (side + 1) * TOK)
            k2_s[ws, part] = dot_nt(x, wk_s[...]).astype(BF16).reshape(last - first, TOK, CP)
            v = dot_nt(wv_s[...], x).astype(BF16)
            for i in range(last - first):
                v2_s[first + i, :, part] = v[:, i * TOK : (i + 1) * TOK]
        every = list(range(first, last))
        attend(every, [k2_s[w] for w in every], [v2_s[w] for w in every], HEADS * DP)
        mixed = [dot(wp_s[...], o_s[w]) for w in every]
        mixed = [m.T[:, :C] for m in mixed]
        for i in range(0, len(every), 2):
            shaped = jnp.stack(mixed[i : i + 2], axis=0).reshape(2, 2, own_rows, WIN, C)
            shaped = shaped.transpose(1, 2, 0, 3, 4).reshape(2, own_rows, 2 * WIN, C)
            cols = slice(every[i] * WIN, every[i] * WIN + 2 * WIN)
            total = x_ref[:, :, cols].astype(F32) + shaped
            att[:, HALO : HALO + own_rows, cols, :C] = total.astype(BF16)

    def halo_copy(side, k):
        first, last = spans[k]
        cols = pl.ds(first * WIN, (last - first) * WIN)
        src_row = own_rows if side else HALO
        dst_row = 0 if side else HALO + own_rows
        return pltpu.make_async_remote_copy(
            src_ref=att.at[:, pl.ds(src_row, HALO), cols],
            dst_ref=att.at[:, pl.ds(dst_row, HALO), cols],
            send_sem=hsend_sem.at[side, k],
            recv_sem=hrecv_sem.at[side, k],
            device_id=(me, ha + (1 if side else -1)),
            device_id_type=MESH,
        )

    def products(field, every, layer, slots, start, stop):
        for first in range(0, len(every), 4):
            product(field, every[first : first + 4], layer, slots, start, stop)

    def product(field, jobs, layer, slots, start, stop):
        stacked = jnp.concatenate(
            [
                jnp.concatenate([field[f, row + r, start:stop] for r in range(3)], axis=1)
                for f, row in jobs
            ],
            axis=0,
        )
        part = dot(stacked, wc_s[layer])
        size = stop - start
        left, middle, right = slots
        for i, (f, row) in enumerate(jobs):
            job = f * (own_rows + 2) + row
            mine = part[i * size : (i + 1) * size]
            left[job, 8 + start : 8 + stop] = mine[:, :CP]
            middle[job, start:stop] = mine[:, CP : 2 * CP]
            right[job, start:stop] = mine[:, 2 * CP :]

    def summed(slots, f, row, start, stop):
        left, middle, right = slots
        job = f * (own_rows + 2) + row
        return (
            middle[job, start:stop]
            + left[job, 7 + start : 7 + stop]
            + right[job, 1 + start : 1 + stop]
        )

    slots1, slots2 = (left1_s, middle1_s, right1_s), (left2_s, middle2_s, right2_s)

    def behind(start, stop):
        return max(0, start - LAG), (stop if stop == width else stop - LAG)

    def grid(rows):
        return [(f, row) for row in rows for f in range(2)]

    def wait_halo(k):
        @pl.when(has_down)
        def _():
            halo_copy(0, k).wait_recv()

        @pl.when(has_up)
        def _():
            halo_copy(1, k).wait_recv()

    def conv_rows(rows1, rows2, start, stop):
        products(att, grid(rows1), 0, slots1, start, stop)
        start, stop = behind(start, stop)
        for f, row in grid(rows1):
            total = jnp.maximum(summed(slots1, f, row, start, stop), 0.0)
            if row == 0:
                total = jnp.where(has_up, total, 0.0)
            if row == own_rows + 1:
                total = jnp.where(has_down, total, 0.0)
            inner[f, row, start:stop] = total.astype(BF16)
        products(inner, grid(rows2), 1, slots2, start, stop)
        start, stop = behind(start, stop)
        for f, row in grid(rows2):
            total = att[f, row + HALO, start:stop].astype(F32)
            total = total + summed(slots2, f, row, start, stop)
            out_ref[f, row, start:stop] = total[:, :C].astype(BF16)

    def conv_inside(start, stop):
        conv_rows(range(2, own_rows), range(2, own_rows - 2), start, stop)

    done = 0
    for k, (first, last) in enumerate(spans):
        if k > 1:
            conv_inside(done, first * WIN)
            done = first * WIN

        @pl.when(has_prev)
        def _(k=k):
            clip_copy(0, k).wait_recv()

        @pl.when(has_next)
        def _(k=k):
            clip_copy(1, k).wait_recv()

        mutual_chunk(first, last)

        @pl.when(has_up)
        def _(k=k):
            halo_copy(0, k).start()

        @pl.when(has_down)
        def _(k=k):
            halo_copy(1, k).start()

    conv_inside(done, width)
    rows1 = (0, 1, own_rows, own_rows + 1)
    rows2 = (0, 1, own_rows - 2, own_rows - 1)
    done = 0
    for group in ((0,), (1, 2), (3, 4)):
        for k in group:
            wait_halo(k)
        conv_rows(rows1, rows2, done, spans[group[-1]][1] * WIN)
        done = spans[group[-1]][1] * WIN

    for k in range(len(spans)):
        for copy, low, high in ((clip_copy, has_next, has_prev), (halo_copy, has_up, has_down)):

            @pl.when(low)
            def _(copy=copy, k=k):
                copy(0, k).wait_send()

            @pl.when(high)
            def _(copy=copy, k=k):
                copy(1, k).wait_send()


def shards(frames, ln_gain, w_qkv, w_proj, conv_weight):
    c, f, h, w = frames.shape
    windows = w // WIN
    clips, parts = lax.axis_size("clip"), lax.axis_size("ha")
    tokens = frames.transpose(1, 2, 3, 0)
    vmem = pl.BlockSpec(memory_space=pltpu.VMEM)
    restored = pl.pallas_call(
        functools.partial(kernel, clips, parts),
        out_shape=jax.ShapeDtypeStruct((f, h, w, c), BF16),
        in_specs=[vmem] * 5,
        out_specs=vmem,
        scratch_shapes=[
            pltpu.VMEM((windows, TOK, CP), BF16),
            pltpu.VMEM((windows * c, TOK), BF16),
            pltpu.VMEM((2, windows * c, TOK), BF16),
            pltpu.VMEM((windows, CP, TOK), BF16),
            pltpu.VMEM((windows, TOK, CP), BF16),
            pltpu.VMEM((windows, HEADS * DP, TOK), BF16),
            pltpu.VMEM((windows, 2 * TOK, CP), BF16),
            pltpu.VMEM((windows, HEADS * DP, 2 * TOK), BF16),
            pltpu.VMEM((windows, 2 * HEADS * DP, TOK), BF16),
            pltpu.VMEM((f, h + 2 * HALO, w, CP), BF16),
            pltpu.VMEM((f, h + 2, w, CP), BF16),
            pltpu.VMEM((CP, CP), BF16),
            pltpu.VMEM((CP, CP), BF16),
            pltpu.VMEM((HEADS * DP, CP), BF16),
            pltpu.VMEM((CP, 2 * HEADS * DP), BF16),
            pltpu.VMEM((2, 3 * CP, 3 * CP), BF16),
            pltpu.VMEM((HEADS, CP, TOK), BF16),
            *[pltpu.VMEM((f * (h + 2), w + 16, CP), F32) for _ in range(6)],
            pltpu.SemaphoreType.DMA((2, len(CUTS))),
            pltpu.SemaphoreType.DMA((2, len(CUTS))),
            pltpu.SemaphoreType.DMA((2, len(CUTS))),
            pltpu.SemaphoreType.DMA((2, len(CUTS))),
        ],
        compiler_params=pltpu.CompilerParams(
            collective_id=0, has_side_effects=True, vmem_limit_bytes=48 * 1024 * 1024
        ),
    )(tokens, ln_gain, w_qkv, w_proj, conv_weight)
    return restored.transpose(3, 0, 1, 2)


def solution(mesh):
    return jax.shard_map(
        shards,
        mesh=mesh,
        in_specs=(P(None, "clip", "ha", None), P(), P(), P(), P()),
        out_specs=P(None, "clip", "ha", None),
        check_vma=False,
    )
```
